128 devices in a mesh: rows: 32 (over x_lo, z, y), cent: 4 (over x_hi, core).
Axes of the slice: x: 4 (x_hi: 2, x_lo: 2; x = x_hi * 2 + x_lo), y: 4, z: 4, core: 2. Of those that a mesh axis runs over, the one named last changes fastest.
Arguments:
- samples: bfloat16 [32768, 512], P('rows'), may hold values from -6 to 6
- weights: float32 [32768], P('rows'), may hold values from 0.2 to 18, as said below
- targets: float32 [16, 32768], P(None, 'rows'), may hold values from -6 to 6
- predictions: float32 [16, 32768], P(None, 'rows'), may hold values from -3 to 3
- centres: bfloat16 [131072, 512], P('rows'), may hold values from -6 to 6
- coefs: float32 [16, 131072], P(None, 'rows'), may hold values from -7 to 7
- block_index: int32 [2, 12288], P(None, 'cent'), may hold values from 0 to 131071, as said below
Outputs:
- new_coefs: float32 [16, 131072], P(None, 'rows')
- new_predictions: float32 [16, 32768], P(None, 'rows')
The draws below stay inside these ranges and needn't reach their ends.
Inputs may be any that keep to these rules, and one draw needn't show every extreme that they name: Positive sample weights. `block_index`: no pool index appears twice in the whole array. In every step each aligned block of 3072 entries starting at a multiple of 3072 takes exactly 96 indices from each pool shard (index // 4096).
All inputs are finite; a program needn't handle non-finite values.
Results may differ from the reference program's by a relative error of at most 0.008.
Values may be sent and summed in bfloat16 or wider, within the bound.
A program may use at most 64 MiB of HBM per device.

```python
import math
import jax
import jax.numpy as jnp
from jax import lax

F = 512
TARGETS = 16
BLOCK = 12288
STEPS = 2
POOL_DEV = 4096
ROWS = 32768
POOL = 131072
SLICE = 3072


def draw_samples(key, part):
    values = jax.random.truncated_normal(key, -6.0, 6.0, (ROWS, F), jnp.float32)
    return values.astype(jnp.bfloat16)


def draw_centres(key, part):
    values = jax.random.truncated_normal(key, -6.0, 6.0, (POOL, F), jnp.float32)
    return values.astype(jnp.bfloat16)


def draw_targets(key, part):
    return jax.random.truncated_normal(key, -6.0, 6.0, (TARGETS, ROWS), jnp.float32)


def draw_coefs(key, part):
    return jax.random.truncated_normal(key, -6.0, 6.0, (TARGETS, POOL), jnp.float32)


def draw_weights(key, part):
    ramp = jnp.arange(ROWS, dtype=jnp.float32) / ROWS
    base = jnp.exp(jax.random.uniform(key, (ROWS,), jnp.float32, math.log(0.3), math.log(3.0)))
    return base * jnp.exp(math.log(3.0) * ramp)


def draw_block_index(key, part):
    owners_count = POOL // POOL_DEV
    slices_count = BLOCK // SLICE
    share = SLICE // owners_count
    taken = STEPS * slices_count * share

    def one_owner(owner_id):
        order = jax.random.permutation(jax.random.fold_in(key, owner_id), POOL_DEV)
        return order[:taken].astype(jnp.int32) + owner_id * POOL_DEV
    chosen = jax.vmap(one_owner)(jnp.arange(owners_count, dtype=jnp.int32))
    chosen = chosen.reshape(owners_count, STEPS, slices_count, share)
    chosen = chosen.transpose(1, 2, 0, 3).reshape(STEPS * slices_count, SLICE)
    mixer = jax.random.fold_in(key, 7919 + owners_count)

    def shuffle(group_id, entries):
        order = jax.random.permutation(jax.random.fold_in(mixer, group_id), SLICE)
        return entries[order]
    mixed = jax.vmap(shuffle)(jnp.arange(STEPS * slices_count, dtype=jnp.int32), chosen)
    return mixed.reshape(STEPS, BLOCK).astype(jnp.int32)


def steps_of(own_key, shape, split, least, top_value):
    factor_of, own = 1.0, jax.random.fold_in(own_key, 6)
    for dim, shards_of in split:
        steps = jnp.exp(jax.random.uniform(jax.random.fold_in(own, dim), (shards_of,), jnp.float32, least / len(split), top_value / len(split)))
        factor_of = factor_of * jnp.repeat(steps, shape[dim] // shards_of).reshape([-1 if axis == dim else 1 for axis in range(len(shape))])
    return factor_of


def scatter_about(key, shape, width, bound, cuts=(), kind=jnp.bfloat16):
    result = width * jax.random.normal(key, shape, jnp.float32)
    if cuts:
        result = result * steps_of(key, shape, cuts, -0.22, 0.18)
    return jnp.clip(result, -bound, bound).astype(kind)


def setup_inputs(seed: int = 0) -> dict:
    keys = jax.random.split(jax.random.key(seed), 8)
    samples = draw_samples(jax.random.fold_in(keys[7], 71), 0)
    weights = draw_weights(jax.random.fold_in(keys[7], 71), 0)
    targets = draw_targets(jax.random.fold_in(keys[7], 71), 0)
    predictions = scatter_about(keys[3], (TARGETS, ROWS), 0.5, 3.0, ((1, 32),), jnp.float32)
    centres = draw_centres(jax.random.fold_in(keys[7], 71), 0)
    coefs = draw_coefs(jax.random.fold_in(keys[7], 71), 0)
    block_index = draw_block_index(jax.random.fold_in(keys[7], 71), 0)
    return dict(samples=samples, weights=weights, targets=targets, predictions=predictions, centres=centres, coefs=coefs, block_index=block_index)


RIDGE = 1.0

def kernel_tile(rows_x, rows_norm, centre_rows, centre_norm, sharpness, offset):
    products = lax.dot_general(rows_x, centre_rows, (((1,), (1,)), ((), ())), preferred_element_type=jnp.float32)
    exponent = offset + sharpness * (2.0 * products - rows_norm[:, None] - centre_norm[None, :])
    return jnp.exp(exponent).astype(jnp.bfloat16)

def reference(samples, weights, targets, predictions, centres, coefs, block_index):
    sharpness = 1.3 / math.sqrt(8.0 * F)
    offset = 2.0 * F * sharpness - 1.5 - 0.5 * math.log(ROWS)
    block_rows = math.gcd(ROWS, 512)
    blocks = ROWS // block_rows
    row_norm = lax.optimization_barrier(jnp.sum(jnp.square(samples.astype(jnp.float32)), axis=1))
    sample_blocks = samples.reshape(blocks, block_rows, F)
    norm_blocks = row_norm.reshape(blocks, block_rows)
    weight_blocks = weights.reshape(blocks, block_rows)
    coef = coefs
    pred = predictions
    for step_idx in range(STEPS):
        chosen_idx = block_index[step_idx]
        chosen = centres[chosen_idx]
        centre_norm = lax.optimization_barrier(jnp.sum(jnp.square(chosen.astype(jnp.float32)), axis=1))
        old_coef = coef[:, chosen_idx]
        weighted = (weights[None, :] * (targets - pred)).astype(jnp.bfloat16)
        weighted_blocks = weighted.reshape(TARGETS, blocks, block_rows).transpose(1, 0, 2)

        def first_pass(carry, item):
            gradient, col_square = carry
            rows_x, rows_norm, row_weight, resid = item
            kernel = kernel_tile(rows_x, rows_norm, chosen, centre_norm, sharpness, offset)
            gradient = gradient + jnp.dot(resid, kernel, preferred_element_type=jnp.float32)
            kernel_wide = kernel.astype(jnp.float32)
            col_square = col_square + lax.optimization_barrier(jnp.sum(row_weight[:, None] * kernel_wide * kernel_wide, axis=0))
            return ((gradient, col_square), None)
        start = (jnp.zeros((TARGETS, BLOCK), jnp.float32), jnp.zeros((BLOCK,), jnp.float32))
        (gradient, col_square), _ = lax.scan(first_pass, start, (sample_blocks, norm_blocks, weight_blocks, weighted_blocks))
        gradient = gradient - RIDGE * old_coef
        delta = gradient / (col_square + RIDGE)[None, :]
        coef = coef.at[:, chosen_idx].add(delta)
        delta_low = delta.astype(jnp.bfloat16)

        def second_pass(carry, item):
            rows_x, rows_norm = item
            kernel = kernel_tile(rows_x, rows_norm, chosen, centre_norm, sharpness, offset)
            change = lax.dot_general(delta_low, kernel, (((1,), (1,)), ((), ())), preferred_element_type=jnp.float32)
            return (carry, change)
        _, changes = lax.scan(second_pass, jnp.zeros((), jnp.float32), (sample_blocks, norm_blocks))
        pred = pred + changes.transpose(1, 0, 2).reshape(TARGETS, ROWS)
    return (coef, pred)
```

```python
import functools
import math

import jax
import jax.numpy as jnp
from jax import lax
from jax.experimental import pallas as pl
from jax.experimental.pallas import tpu as pltpu
from jax.sharding import PartitionSpec as P

RIDGE = 1.0
MESH = pl.DeviceIdType.MESH
F32, BF16 = jnp.float32, jnp.bfloat16
LOG2E = 1.4426950408889634
NT = (((1,), (1,)), ((), ()))


def extract(scale, blk, centres, coefs, samples, weights, targets, preds,
            picked, own_coef, place, weighted, aux, samples_t, select):
    pool = centres.shape[0]
    first = lax.axis_index("rows") * pool
    q_rows = blk.shape[1]
    upper = (lax.broadcasted_iota(jnp.int32, (128, 128), 0)
             <= lax.broadcasted_iota(jnp.int32, (128, 128), 1)).astype(F32)
    lower = (lax.broadcasted_iota(jnp.int32, (q_rows, q_rows), 0)
             > lax.broadcasted_iota(jnp.int32, (q_rows, q_rows), 1)).astype(F32)
    rank_of = lax.broadcasted_iota(jnp.int32, (128, 128), 0).astype(F32)
    coef = coefs[...]
    hi = coef.astype(BF16)
    rest = coef - hi.astype(F32)
    mid = rest.astype(BF16)
    low = (rest - mid.astype(F32)).astype(BF16)
    parts = jnp.concatenate([hi, mid, low], axis=0)
    for s in range(2):
        local = blk[s] - first
        mine = jnp.logical_and(local >= 0, local < pool)
        flag = mine.astype(F32)
        inner = jnp.dot(flag, upper, preferred_element_type=F32)
        before = jnp.sum(jnp.dot(lower, flag, preferred_element_type=F32), axis=1, keepdims=True)
        rank = jnp.where(mine, inner + before - 1.0, -1.0)
        local_f = local.astype(F32)
        acc = jnp.zeros((128, 128), F32)
        for q in range(q_rows):
            acc = acc + jnp.where(rank[q : q + 1, :] == rank_of, local_f[q : q + 1, :], 0.0)
        col = jnp.sum(acc, axis=1, keepdims=True)
        row = jnp.sum(acc.T, axis=0, keepdims=True)
        valid = lax.broadcasted_iota(jnp.int32, (128, 1), 0) < 96
        col = jnp.where(valid, col, -1.0)
        row = jnp.where(lax.broadcasted_iota(jnp.int32, (1, 128), 1) < 96, row, -1.0)
        place[s] = jnp.broadcast_to(row, (8, 128))
        for k in range(0, pool, 512):
            lanes = (lax.broadcasted_iota(jnp.int32, (128, 512), 1) + k).astype(F32)
            select[s * 128 : (s + 1) * 128, k : k + 512] = (col == lanes).astype(F32).astype(BF16)
        three = lax.dot_general(parts, select[s * 128 : (s + 1) * 128, :], NT,
                                preferred_element_type=F32)
        own_coef[s] = three[0:16] + three[16:32] + three[32:48]
    rows = jnp.dot(select[...], centres[...], preferred_element_type=F32).astype(BF16)
    picked[0] = rows[0:96]
    picked[1] = rows[128:224]
    x = samples[...]
    samples_t[...] = x.T
    xf = x.astype(F32)
    sq = xf * xf
    sq_hi = sq.astype(BF16)
    sq_lo = (sq - sq_hi.astype(F32)).astype(BF16)
    ones = jnp.ones((16, x.shape[1]), BF16)
    norm = (lax.dot_general(ones, sq_hi, NT, preferred_element_type=F32)
            + lax.dot_general(ones, sq_lo, NT, preferred_element_type=F32))
    w = weights[...]
    aux[...] = jnp.zeros_like(aux)
    aux[0:1, :] = w
    aux[1:2, :] = -scale * norm[0:1, :]
    weighted[...] = (w * (targets[...] - preds[...])).astype(BF16)


def main_kernel(scale, shift, picked, own_coef, place, weighted, aux, samples_t, targets, preds, coefs,
                pred_out, coef_out,
                cent, peer_t, peer_coef, places, wt, peer_wt, auxes, wcat, kt, gpart, grecv, dlow, dall,
                ppart, precv, wt2, pfin,
                xs, xr, cs, cr, gs, gr, ds_, dr, fs, fr, ps, pr, ws, wr, qs, qr, ls, lr):
    r = lax.axis_index("rows")
    c = lax.axis_index("cent")
    xl = r // 16
    me = lax.rem(r, 16)
    z = me // 4
    y = lax.rem(me, 4)
    e = xl * 4 + c

    def wrap(v):
        return lax.rem(v + 8, 4)

    def plane_dev(j):
        return (xl * 16 + j, c)

    def ring_dev(k):
        return ((k // 4) * 16 + me, lax.rem(k, 4))

    barrier = pltpu.get_barrier_semaphore()

    def greet_plane(k, carry):
        pl.semaphore_signal(barrier, inc=1, device_id=plane_dev(lax.rem(me + k, 16)), device_id_type=MESH)
        return carry

    def greet_ring(k, carry):
        pl.semaphore_signal(barrier, inc=1, device_id=ring_dev(lax.rem(e + k, 8)), device_id_type=MESH)
        return carry

    lax.fori_loop(1, 16, greet_plane, 0)
    lax.fori_loop(1, 8, greet_ring, 0)
    pl.semaphore_wait(barrier, 22)

    def remote(src, dst, ssem, rsem, dev):
        return pltpu.make_async_remote_copy(src_ref=src, dst_ref=dst, send_sem=ssem, recv_sem=rsem,
                                            device_id=dev, device_id_type=MESH)

    partner = ((1 - xl) * 16 + me, c)
    across = ((1 - xl) * 16 + me, lax.rem(c + 2, 4))

    def half_copy(s):
        return remote(picked.at[s, pl.ds(48, 48)], cent.at[s, me, pl.ds(48, 48)], xs.at[s], xr.at[s], partner)

    cut = 224
    depth = samples_t.shape[0]
    x_copies = [
        remote(aux, auxes.at[1], xs.at[2], xr.at[2], partner),
        remote(weighted, peer_wt, xs.at[3], xr.at[3], partner),
        remote(samples_t.at[pl.ds(0, cut)], peer_t.at[pl.ds(0, cut)], xs.at[4], xr.at[4], partner),
        remote(samples_t.at[pl.ds(cut, depth - cut)], peer_t.at[pl.ds(cut, depth - cut)], xs.at[5], xr.at[5],
               across),
        remote(own_coef, peer_coef, xs.at[6], xr.at[6], partner),
    ]
    half_copy(0).start()
    half_copy(1).start()

    counters = [0, 0]

    def slot(part, a, b):
        if part == 0:
            return wrap(z + b) * 4 + wrap(y + a)
        return wrap(z + a) * 4 + wrap(y + b)

    started = [[], []]

    def send(s, part, j, a, b):
        n = counters[s]
        counters[s] += 1
        ref = cent.at[s, j, pl.ds(48 * part, 48)]
        cp = remote(ref, ref, cs.at[s, n], cr.at[s, part, j], plane_dev(slot(part, a, b)))
        cp.start()
        started[s].append(cp)

    def got(s, part, j):
        ref = cent.at[s, j, pl.ds(48 * part, 48)]
        remote(ref, ref, cs.at[s, 0], cr.at[s, part, j], plane_dev(slot(part, 1, 0))).wait_recv()

    def launch(s, part):
        for a, b in ((1, 0), (-1, 0), (0, 1), (0, -1)):
            send(s, part, me, a, b)

    for s in range(2):
        cent[s, me, 0:48] = picked[s, 0:48]
    for s in range(2):
        launch(s, 0)
    for cp in x_copies:
        cp.start()

    def share_place(k, carry):
        to = lax.rem(c + k, 4)
        remote(place, places.at[c], ls.at[k], lr.at[c], (r, to)).start()
        return carry

    lax.fori_loop(1, 4, share_place, 0)
    places[c] = place[...]

    def events(s):
        out = []

        def first(part):
            half_copy(s).wait_recv()
            launch(s, part)

        out.append(lambda: first(1))

        def near(part, sign, fwd):
            j = slot(part, -sign, 0)
            got(s, part, j)
            if fwd:
                send(s, part, j, sign, 0)
            send(s, part, j, 0, 1)
            send(s, part, j, 0, -1)

        def far(part):
            j = slot(part, 2, 0)
            got(s, part, j)
            send(s, part, j, 0, 1)
            send(s, part, j, 0, -1)

        def second(part, d, sign):
            j = slot(part, d, -sign)
            got(s, part, j)
            if (sign == 1) == (d in (0, 3)):
                send(s, part, j, 0, sign)

        def last(part, d):
            got(s, part, slot(part, d, 2))

        for part in (0, 1):
            for sign in (1, -1):
                out.append(functools.partial(near, part, sign, (sign == 1) == (s == part)))
        for d in (0, -1, 1, 2):
            if d == 2:
                out.append(functools.partial(far, 0))
                out.append(functools.partial(far, 1))
            for part in (0, 1):
                for sign in (1, -1):
                    out.append(functools.partial(second, part, d % 4, sign))
        for d in range(4):
            for part in (0, 1):
                out.append(functools.partial(last, part, d))
        return out

    auxes[0] = aux[...]
    wt[:, 0:1024] = weighted[...]
    for s in range(2):
        for j in range(16):
            kt[s, j, 96:128, :] = jnp.zeros((32, 2048), BF16)

    def tiles(s, half, groups):
        src = samples_t if half == 0 else peer_t

        def body(g, carry):
            rows = cent[s, pl.ds(g * 4, 4)].reshape(384, 512)
            wide = rows.astype(F32)
            a = shift - scale * jnp.sum(wide * wide, axis=1, keepdims=True)
            for i in range(4):
                prod = jnp.dot(rows, src[:, i * 256 : (i + 1) * 256], preferred_element_type=F32)
                b = auxes[half, 1:2, i * 256 : (i + 1) * 256]
                val = jnp.exp2(prod * (2.0 * scale) + (a + b)).astype(BF16)
                lo = half * 1024 + i * 256
                for q in range(4):
                    kt[s, g * 4 + q, 0:96, lo : lo + 256] = val[q * 96 : (q + 1) * 96]
            return carry

        lax.fori_loop(groups[0], groups[1], body, 0)

    def squares(s, pairs):
        def body(j2, carry):
            k = kt[s, pl.ds(j2 * 2, 2)].reshape(256, 2048)
            sq = lax.dot_general(wcat[...], k * k, NT, preferred_element_type=F32)
            tot = jnp.broadcast_to(sq[0:1] + sq[1:2], (8, 256))
            gpart[s, j2 * 2, 16:24] = tot[:, 0:128]
            gpart[s, j2 * 2 + 1, 16:24] = tot[:, 128:256]
            return carry

        lax.fori_loop(pairs[0], pairs[1], body, 0)

    def g_copy(s, j):
        return remote(gpart.at[s, j], grecv.at[s, me], gs.at[s, j], gr.at[s, me], plane_dev(j))

    def gradient(s, rhs):
        def pair(j2):
            k = kt[s, pl.ds(j2 * 2, 2)].reshape(256, 2048)
            g = lax.dot_general(rhs, k, NT, preferred_element_type=F32)
            gpart[s, j2 * 2, 0:16] = g[:, 0:128]
            gpart[s, j2 * 2 + 1, 0:16] = g[:, 128:256]

        def body(k, carry):
            j2 = lax.rem(me // 2 + k, 8)
            pair(j2)
            g_copy(s, j2 * 2).start()
            g_copy(s, j2 * 2 + 1).start()
            return carry

        lax.fori_loop(1, 8, body, 0)
        pair(me // 2)
        g_copy(s, me + 1 - 2 * lax.rem(me, 2)).start()

    def d_copy(s, j):
        return remote(dlow.at[s, me], dlow.at[s, me], ds_.at[s, j], dr.at[s, me], plane_dev(j))

    def f_copy(s, k):
        return remote(dall.at[s, e], dall.at[s, e], fs.at[s, k], fr.at[s, e], ring_dev(k))

    def make_delta(s):
        total = gpart[s, me]

        def body(k, total):
            j = lax.rem(me + k, 16)
            remote(gpart.at[s, j], grecv.at[s, j], gs.at[s, j], gr.at[s, j], plane_dev(j)).wait_recv()
            return total + grecv[s, j]

        total = lax.fori_loop(1, 16, body, total)
        lane = lax.broadcasted_iota(jnp.int32, (16, 128), 1)
        coef = jnp.where(lane < 48, own_coef[s], peer_coef[s])
        delta = (total[0:16] - RIDGE * coef) / (total[16:17] + RIDGE)
        dlow[s, me] = delta.astype(BF16)
        dall[s, e] = delta

        def push(k, carry):
            d_copy(s, lax.rem(me + k, 16)).start()
            return carry

        lax.fori_loop(1, 16, push, 0)

        def push_ring(k, carry):
            f_copy(s, lax.rem(e + k, 8)).start()
            return carry

        lax.fori_loop(1, 8, push_ring, 0)

    def wait_delta(s):
        def body(k, carry):
            j = lax.rem(me + k, 16)
            remote(dlow.at[s, j], dlow.at[s, j], ds_.at[s, j], dr.at[s, j], plane_dev(j)).wait_recv()
            return carry

        lax.fori_loop(1, 16, body, 0)

    def p_copy(s, to):
        return remote(ppart.at[s, to], precv.at[s, e], ps.at[s, to], pr.at[s, e], ring_dev(to))

    def change(s):
        d = jnp.concatenate([dlow[s, j] for j in range(16)], axis=1)

        def chunk(to):
            rel = lax.rem(to // 4 + xl, 2) * 4 + lax.rem(to, 4)
            k = kt[s, :, :, pl.ds(pl.multiple_of(rel * 256, 256), 256)].reshape(2048, 256)
            ppart[s, to] = jnp.dot(d, k, preferred_element_type=F32)

        def body(k, carry):
            to = lax.rem(e + k, 8)
            chunk(to)
            p_copy(s, to).start()
            return carry

        lax.fori_loop(1, 8, body, 0)
        chunk(e)

    def sum_change(s):
        def body(k, total):
            j = lax.rem(e + k, 8)
            remote(ppart.at[s, j], precv.at[s, j], ps.at[s, j], pr.at[s, j], ring_dev(j)).wait_recv()
            return total + precv[s, j]

        return lax.fori_loop(1, 8, body, ppart[s, e])

    def update_coefs(s, base):
        def body(k, carry):
            j = lax.rem(e + k, 8)
            remote(dall.at[s, j], dall.at[s, j], fs.at[s, j], fr.at[s, j], ring_dev(j)).wait_recv()
            return carry

        lax.fori_loop(1, 8, body, 0)
        lane = lax.broadcasted_iota(jnp.int32, (16, 128), 1)
        pieces, cols = [], []
        for k in range(4):
            own = dall[s, xl * 4 + k]
            other = dall[s, (1 - xl) * 4 + k]
            pieces.append(jnp.where(lane < 48, own, other))
            row = places[k, s, 0:1]
            cols.append(jnp.broadcast_to(row, (128, 128)).T)
        d = jnp.concatenate(pieces, axis=1)
        hi = d.astype(BF16)
        rest = d - hi.astype(F32)
        mid = rest.astype(BF16)
        low = (rest - mid.astype(F32)).astype(BF16)
        lhs = jnp.concatenate([hi, mid, low], axis=0)
        col = jnp.concatenate(cols, axis=0)

        def step(k, carry):
            at = pl.ds(pl.multiple_of(k * 512, 512), 512)
            base_lane = (k * 512).astype(F32)
            hot = []
            for i in range(4):
                lanes = lax.broadcasted_iota(jnp.int32, (512, 128), 1).astype(F32) + (base_lane + i * 128.0)
                hot.append((col == lanes).astype(F32).astype(BF16))
            three = jnp.dot(lhs, jnp.concatenate(hot, axis=1), preferred_element_type=F32)
            coef_out[:, at] = base[:, at] + (three[0:16] + three[16:32] + three[32:48])
            return carry

        lax.fori_loop(0, 8, step, 0)

    for ev in events(0):
        ev()
    x_copies[0].wait_recv()
    w2 = jnp.concatenate([auxes[0, 0:1], auxes[1, 0:1]], axis=1)
    w_hi = w2.astype(BF16).astype(F32)
    row_id = lax.broadcasted_iota(jnp.int32, (16, 2048), 0)
    wcat[...] = jnp.where(row_id == 0, w_hi, jnp.where(row_id == 1, w2 - w_hi, 0.0)).astype(BF16)
    later = events(1)
    cuts = [0, 7, 14, 21, len(later)]
    tiles(0, 0, (0, 2))
    for ev in later[: cuts[1]]:
        ev()
    tiles(0, 0, (2, 4))
    for ev in later[cuts[1] : cuts[2]]:
        ev()
    x_copies[2].wait_recv()
    x_copies[3].wait_recv()
    tiles(0, 1, (0, 2))
    for ev in later[cuts[2] : cuts[3]]:
        ev()
    tiles(0, 1, (2, 4))
    squares(0, (0, 8))
    x_copies[1].wait_recv()
    x_copies[4].wait_recv()
    wt[:, 1024:2048] = peer_wt[...]
    gradient(0, wt[...])
    for ev in later[cuts[3] :]:
        ev()
    tiles(1, 0, (0, 4))
    make_delta(0)
    tiles(1, 1, (0, 4))
    wait_delta(0)
    change(0)
    squares(1, (0, 8))

    def wait_place(k, carry):
        j = lax.rem(c + k, 4)
        remote(place, places.at[j], ls.at[k], lr.at[j], (r, j)).wait_recv()
        return carry

    lax.fori_loop(1, 4, wait_place, 0)
    chunk_at = pl.ds(pl.multiple_of(c * 256, 256), 256)
    pred = preds[:, chunk_at] + sum_change(0)

    def rel_to(to):
        return lax.rem(to // 4 + xl, 2) * 4 + c

    def w_copy(to):
        return remote(wt2.at[c], wt2.at[rel_to(to)], ws.at[to], wr.at[rel_to(to)], ring_dev(to))

    wt2[c] = (auxes[0, 0:1, chunk_at] * (targets[:, chunk_at] - pred)).astype(BF16)

    def push_w(k, carry):
        w_copy(lax.rem(e + k, 8)).start()
        return carry

    lax.fori_loop(1, 8, push_w, 0)
    update_coefs(0, coefs)

    def wait_w(k, carry):
        j = lax.rem(c + k, 8)
        remote(wt2.at[j], wt2.at[j], ws.at[j], wr.at[j], ring_dev(j)).wait_recv()
        return carry

    lax.fori_loop(1, 8, wait_w, 0)
    gradient(1, jnp.concatenate([wt2[j] for j in range(8)], axis=1))
    make_delta(1)
    wait_delta(1)
    change(1)
    update_coefs(1, coef_out)
    pfin[c] = pred + sum_change(1)

    def q_copy(k):
        to = lax.rem(c + k, 4)
        return remote(pfin.at[c], pfin.at[c], qs.at[to], qr.at[c], (r, to))

    def push_q(k, carry):
        q_copy(k).start()
        return carry

    def wait_q(k, carry):
        j = lax.rem(c + k, 4)
        remote(pfin.at[j], pfin.at[j], qs.at[j], qr.at[j], (r, j)).wait_recv()
        return carry

    lax.fori_loop(1, 4, push_q, 0)
    lax.fori_loop(1, 4, wait_q, 0)
    for k in range(4):
        pred_out[:, k * 256 : (k + 1) * 256] = pfin[k]

    for s in range(2):
        half_copy(s).wait_send()
        for cp in started[s]:
            cp.wait_send()
    for cp in x_copies:
        cp.wait_send()

    def drain_plane(k, carry):
        j = lax.rem(me + k, 16)
        for s in range(2):
            g_copy(s, j).wait_send()
            d_copy(s, j).wait_send()
        return carry

    def drain_ring(k, carry):
        j = lax.rem(e + k, 8)
        for s in range(2):
            f_copy(s, j).wait_send()
            p_copy(s, j).wait_send()
        w_copy(j).wait_send()
        return carry

    def drain_cent(k, carry):
        q_copy(k).wait_send()
        remote(place, places.at[c], ls.at[k], lr.at[c], (r, lax.rem(c + k, 4))).wait_send()
        return carry

    lax.fori_loop(1, 16, drain_plane, 0)
    lax.fori_loop(1, 8, drain_ring, 0)
    lax.fori_loop(1, 4, drain_cent, 0)


def local(samples, weights, targets, predictions, centres, coefs, block_index):
    rows, depth = samples.shape
    pool = centres.shape[0]
    t = targets.shape[0]
    sharpness = 1.3 / math.sqrt(8.0 * depth)
    offset = 2.0 * depth * sharpness - 1.5 - 0.5 * math.log(rows * lax.axis_size("rows"))
    scale = sharpness * LOG2E
    shift = offset * LOG2E
    vmem = pl.BlockSpec(memory_space=pltpu.VMEM)
    sds = jax.ShapeDtypeStruct
    prepared = pl.pallas_call(
        functools.partial(extract, scale),
        out_shape=(
            sds((2, 96, depth), BF16),
            sds((2, t, 128), F32),
            sds((2, 8, 128), F32),
            sds((t, rows), BF16),
            sds((8, rows), F32),
            sds((depth, rows), BF16),
        ),
        in_specs=[vmem] * 7,
        out_specs=(vmem,) * 6,
        scratch_shapes=[pltpu.VMEM((256, pool), BF16)],
        compiler_params=pltpu.CompilerParams(vmem_limit_bytes=40 * 2**20),
    )(block_index.reshape(2, -1, 128), centres, coefs, samples, weights[None, :], targets, predictions)
    dma = pltpu.SemaphoreType.DMA
    pred, coef = pl.pallas_call(
        functools.partial(main_kernel, scale, shift),
        out_shape=(sds((t, rows), F32), sds((t, pool), F32)),
        in_specs=[vmem] * 9,
        out_specs=(vmem,) * 2,
        scratch_shapes=[
            pltpu.VMEM((2, 16, 96, depth), BF16),
            pltpu.VMEM((depth, rows), BF16),
            pltpu.VMEM((2, t, 128), F32),
            pltpu.VMEM((4, 2, 8, 128), F32),
            pltpu.VMEM((t, 2 * rows), BF16),
            pltpu.VMEM((t, rows), BF16),
            pltpu.VMEM((2, 8, rows), F32),
            pltpu.VMEM((16, 2 * rows), BF16),
            pltpu.VMEM((2, 16, 128, 2 * rows), BF16),
            pltpu.VMEM((2, 16, 24, 128), F32),
            pltpu.VMEM((2, 16, 24, 128), F32),
            pltpu.VMEM((2, 16, t, 128), BF16),
            pltpu.VMEM((2, 8, t, 128), F32),
            pltpu.VMEM((2, 8, t, 256), F32),
            pltpu.VMEM((2, 8, t, 256), F32),
            pltpu.VMEM((8, t, 256), BF16),
            pltpu.VMEM((4, t, 256), F32),
            dma((7,)), dma((7,)),
            dma((2, 30)), dma((2, 2, 16)),
            dma((2, 16)), dma((2, 16)),
            dma((2, 16)), dma((2, 16)),
            dma((2, 8)), dma((2, 8)),
            dma((2, 8)), dma((2, 8)),
            dma((8,)), dma((8,)),
            dma((4,)), dma((4,)),
            dma((4,)), dma((4,)),
        ],
        compiler_params=pltpu.CompilerParams(
            collective_id=0, has_side_effects=True, vmem_limit_bytes=48 * 2**20
        ),
    )(*prepared, targets, predictions, coefs)
    return coef, pred


def solution(mesh):
    in_specs = (
        P("rows", None),
        P("rows"),
        P(None, "rows"),
        P(None, "rows"),
        P("rows", None),
        P(None, "rows"),
        P(None, "cent"),
    )
    out_specs = (P(None, "rows"), P(None, "rows"))
    return jax.shard_map(local, mesh=mesh, in_specs=in_specs, out_specs=out_specs, check_vma=False)
```

```python
import functools
import math

import jax
import jax.numpy as jnp
from jax import lax
from jax.experimental import pallas as pl
from jax.experimental.pallas import tpu as pltpu
from jax.sharding import PartitionSpec as P

RIDGE = 1.0
MESH = pl.DeviceIdType.MESH
F32, BF16 = jnp.float32, jnp.bfloat16
LOG2E = 1.4426950408889634
NT = (((1,), (1,)), ((), ()))


def iota(shape, axis):
    return lax.broadcasted_iota(jnp.int32, shape, axis)


def split3(v):
    hi = v.astype(BF16)
    rest = v - hi.astype(F32)
    mid = rest.astype(BF16)
    low = (rest - mid.astype(F32)).astype(BF16)
    return jnp.concatenate([hi, mid, low], axis=0)


def sum3(v):
    return v[0:16] + v[16:32] + v[32:48]


def main_kernel(scale, shift, blk_in, centres_in, coefs_in, samples_in, weights_in, targets_in, preds_in,
                pred_out, coef_out,
                blk, centres, coefs, samples, weights, targets, preds, select,
                outgoing, own_coef, place, weighted, samples_t,
                cent, peer_t, peer_coef, places, wt, peer_wt, auxes, wcat, kt, gsend, grecv, sqsend, sqrecv,
                dlow, dall, psend, precv, lsend, lrecv, wt2, pmid, pend,
                loads, xs, xr, cs, cr, gs, gr, ss, sr, ds_, dr, fs, fr, ps, pr, es, er, ws, wr, qs, qr, ls, lr,
                hs, hr):
    r = lax.axis_index("rows")
    c = lax.axis_index("cent")
    xl = r // 16
    me = lax.rem(r, 16)
    z = me // 4
    y = lax.rem(me, 4)
    e = xl * 4 + c
    core = lax.rem(c, 2)

    def wrap(v):
        return lax.rem(v + 8, 4)

    def plane_dev(j):
        return (xl * 16 + j, c)

    def ring_dev(k):
        return ((k // 4) * 16 + me, lax.rem(k, 4))

    pairs = ((blk_in, blk), (centres_in, centres), (samples_in, samples), (coefs_in, coefs),
             (weights_in, weights), (targets_in, targets), (preds_in, preds))
    fetch = [pltpu.make_async_copy(src, dst, loads.at[i]) for i, (src, dst) in enumerate(pairs)]
    for cp in fetch:
        cp.start()

    barrier = pltpu.get_barrier_semaphore()

    def greet_plane(k, carry):
        pl.semaphore_signal(barrier, inc=1, device_id=plane_dev(lax.rem(me + k, 16)), device_id_type=MESH)
        return carry

    def greet_ring(k, carry):
        pl.semaphore_signal(barrier, inc=1, device_id=ring_dev(lax.rem(e + k, 8)), device_id_type=MESH)
        return carry

    lax.fori_loop(1, 16, greet_plane, 0)
    lax.fori_loop(1, 8, greet_ring, 0)

    pool = centres.shape[0]
    q_rows = blk.shape[1] // 128
    upper = (iota((128, 128), 0) <= iota((128, 128), 1)).astype(F32)
    lower = (iota((q_rows, q_rows), 0) > iota((q_rows, q_rows), 1)).astype(F32)
    rank_of = iota((128, 128), 0).astype(F32)
    fetch[0].wait()
    for s in range(2):
        index = jnp.concatenate([blk[s : s + 1, q * 128 : (q + 1) * 128] for q in range(q_rows)], axis=0)
        at = index - r * pool
        mine = jnp.logical_and(at >= 0, at < pool)
        flag = mine.astype(F32)
        inner = jnp.dot(flag, upper, preferred_element_type=F32)
        before = jnp.sum(jnp.dot(lower, flag, preferred_element_type=F32), axis=1, keepdims=True)
        rank = jnp.where(mine, inner + before - 1.0, -1.0)
        at_f = at.astype(F32)
        acc = jnp.zeros((128, 128), F32)
        for q in range(q_rows):
            acc = acc + jnp.where(rank[q : q + 1, :] == rank_of, at_f[q : q + 1, :], 0.0)
        col = jnp.where(iota((128, 1), 0) < 96, jnp.sum(acc, axis=1, keepdims=True), -1.0)
        row = jnp.where(iota((1, 128), 1) < 96, jnp.sum(acc.T, axis=0, keepdims=True), -1.0)
        place[s] = jnp.broadcast_to(row, (8, 128))
        for k in range(0, pool, 512):
            lanes = (iota((128, 512), 1) + k).astype(F32)
            select[s * 128 : (s + 1) * 128, k : k + 512] = (col == lanes).astype(F32).astype(BF16)
    fetch[1].wait()
    rows = jnp.dot(select[...], centres[...], preferred_element_type=F32).astype(BF16)
    for s in range(2):
        cent[s, me, 0:48] = rows[s * 128 : s * 128 + 48]
        outgoing[s] = rows[s * 128 + 48 : s * 128 + 96]
    fetch[2].wait()
    samples_t[...] = samples[...].T

    pl.semaphore_wait(barrier, 22)

    def remote(src, dst, ssem, rsem, dev):
        return pltpu.make_async_remote_copy(src_ref=src, dst_ref=dst, send_sem=ssem, recv_sem=rsem,
                                            device_id=dev, device_id_type=MESH)

    partner = ((1 - xl) * 16 + me, c)
    across = ((1 - xl) * 16 + me, lax.rem(c + 2, 4))
    sibling = (r, c + 1 - 2 * core)

    def half_copy(s):
        return remote(outgoing.at[s], cent.at[s, me, pl.ds(48, 48)], xs.at[s], xr.at[s], partner)

    counters = [0, 0]
    started = [[], []]

    def slot(part, a, b):
        if part == 0:
            return wrap(z + b) * 4 + wrap(y + a)
        return wrap(z + a) * 4 + wrap(y + b)

    def send(s, part, j, a, b):
        n = counters[s]
        counters[s] += 1
        ref = cent.at[s, j, pl.ds(48 * part, 48)]
        cp = remote(ref, ref, cs.at[s, n], cr.at[s, part, j], plane_dev(slot(part, a, b)))
        cp.start()
        started[s].append(cp)

    def got(s, part, j):
        ref = cent.at[s, j, pl.ds(48 * part, 48)]
        remote(ref, ref, cs.at[s, 0], cr.at[s, part, j], plane_dev(slot(part, 1, 0))).wait_recv()

    def launch(s, part):
        for a, b in ((1, 0), (-1, 0), (0, 1), (0, -1)):
            send(s, part, me, a, b)

    def near(s, part, sign):
        j = slot(part, -sign, 0)
        got(s, part, j)
        if (sign == 1) == (s == part):
            send(s, part, j, sign, 0)
        send(s, part, j, 0, 1)
        send(s, part, j, 0, -1)

    def far(s, part):
        j = slot(part, 2, 0)
        got(s, part, j)
        send(s, part, j, 0, 1)
        send(s, part, j, 0, -1)

    def second(s, part, d, sign):
        j = slot(part, d, -sign)
        got(s, part, j)
        if (sign == 1) == (d in (0, -1)):
            send(s, part, j, 0, sign)

    def last(s, part, d):
        got(s, part, slot(part, d, 2))

    def level(s, n):
        if n == 1:
            for part in (0, 1):
                near(s, part, 1)
                near(s, part, -1)
            for part in (0, 1):
                second(s, part, 0, 1)
                second(s, part, 0, -1)
        elif n == 2:
            for part in (0, 1):
                far(s, part)
            for part in (0, 1):
                for d in (1, -1):
                    second(s, part, d, 1)
                    second(s, part, d, -1)
            for part in (0, 1):
                last(s, part, 0)
        elif n == 3:
            for part in (0, 1):
                second(s, part, 2, 1)
                second(s, part, 2, -1)
            for part in (0, 1):
                last(s, part, 1)
                last(s, part, -1)
        else:
            for part in (0, 1):
                last(s, part, 2)

    half_copy(0).start()
    launch(0, 0)
    half_copy(1).start()

    cut = 112
    depth = samples_t.shape[0]
    low_f = pl.ds(pl.multiple_of(core * 256, 16), cut)
    high_f = pl.ds(pl.multiple_of(core * 256 + cut, 16), 256 - cut)
    sib_low = pl.ds(pl.multiple_of((1 - core) * 256, 16), cut)
    sib_high = pl.ds(pl.multiple_of((1 - core) * 256 + cut, 16), 256 - cut)
    x_samples = [
        remote(samples_t.at[low_f], peer_t.at[low_f], xs.at[2], xr.at[2], partner),
        remote(samples_t.at[high_f], peer_t.at[high_f], xs.at[3], xr.at[3], across),
    ]
    for cp in x_samples:
        cp.start()
    hand = [
        remote(peer_t.at[low_f], peer_t.at[low_f], hs.at[0], hr.at[0], sibling),
        remote(peer_t.at[high_f], peer_t.at[high_f], hs.at[1], hr.at[1], sibling),
    ]
    hand_in = [
        remote(peer_t.at[sib_low], peer_t.at[sib_low], hs.at[0], hr.at[0], sibling),
        remote(peer_t.at[sib_high], peer_t.at[sib_high], hs.at[1], hr.at[1], sibling),
    ]

    for i in (4, 5, 6):
        fetch[i].wait()
    xf = samples[...].astype(F32)
    sq = xf * xf
    sq_hi = sq.astype(BF16)
    sq_lo = (sq - sq_hi.astype(F32)).astype(BF16)
    ones = jnp.ones((16, depth), BF16)
    norm = (lax.dot_general(ones, sq_hi, NT, preferred_element_type=F32)
            + lax.dot_general(ones, sq_lo, NT, preferred_element_type=F32))
    w = weights[...]
    auxes[0] = jnp.where(iota((8, 1024), 0) == 0, w, -scale * norm[0:8])
    weighted[...] = (w * (targets[...] - preds[...])).astype(BF16)
    wt[:, 0:1024] = weighted[...]

    def weight_rows(half):
        v = auxes[half, 0:1]
        hi = v.astype(BF16).astype(F32)
        which = iota((16, 1024), 0)
        full = jnp.where(which == 0, hi, jnp.where(which == 1, v - hi, 0.0))
        wcat[:, half * 1024 : (half + 1) * 1024] = full.astype(BF16)

    weight_rows(0)
    x_rows = [
        remote(auxes.at[0], auxes.at[1], xs.at[4], xr.at[4], partner),
        remote(weighted, peer_wt, xs.at[5], xr.at[5], partner),
    ]
    for cp in x_rows:
        cp.start()

    half_copy(0).wait_recv()
    launch(0, 1)

    fetch[3].wait()
    parts = split3(coefs[...])
    for s in range(2):
        own_coef[s] = sum3(lax.dot_general(parts, select[s * 128 : (s + 1) * 128, :], NT,
                                           preferred_element_type=F32))
    x_coef = remote(own_coef, peer_coef, xs.at[6], xr.at[6], partner)
    x_coef.start()

    def l_copy(k):
        return remote(place, places.at[c], ls.at[k], lr.at[c], (r, lax.rem(c + k, 4)))

    def share_place(k, carry):
        l_copy(k).start()
        return carry

    lax.fori_loop(1, 4, share_place, 0)
    places[c] = place[...]

    def tiles(s, half, first, stop):
        src = samples_t if half == 0 else peer_t
        base = half * 1024

        def body(k, carry):
            g = lax.rem(z + k + k // 2 - 2 * (k // 3), 4)
            picked = cent[s, pl.ds(g * 4, 4)].reshape(384, 512)
            wide = picked.astype(F32)
            a = shift - scale * jnp.sum(wide * wide, axis=1, keepdims=True)
            for i in range(4):
                prod = jnp.dot(picked, src[:, i * 256 : (i + 1) * 256], preferred_element_type=F32)
                b = auxes[half, 1:2, i * 256 : (i + 1) * 256]
                val = jnp.exp2(prod * (2.0 * scale) + (a + b)).astype(BF16)
                lo = base + i * 256
                for q in range(4):
                    kt[s, g * 4 + q, 0:96, lo : lo + 256] = val[q * 96 : (q + 1) * 96]
            for q in (0, 2):
                k2 = kt[s, pl.ds(g * 4 + q, 2), :, base : base + 1024].reshape(256, 1024)
                part = lax.dot_general(wcat[:, base : base + 1024], k2 * k2, NT, preferred_element_type=F32)
                tot = jnp.broadcast_to(part[0:1] + part[1:2], (8, 256))
                for h in range(2):
                    now = tot[:, h * 128 : (h + 1) * 128]
                    if half == 0:
                        sqsend[s, g * 4 + q + h] = now
                    else:
                        sqsend[s, g * 4 + q + h] += now
            return carry

        lax.fori_loop(first, stop, body, 0)

    def s_copy(s, j):
        return remote(sqsend.at[s, j], sqrecv.at[s, me], ss.at[s, j], sr.at[s, me], plane_dev(j))

    def push_squares(s):
        def body(k, carry):
            s_copy(s, lax.rem(me + k, 16)).start()
            return carry

        lax.fori_loop(1, 16, body, 0)

    def g_copy(s, j):
        return remote(gsend.at[s, j], grecv.at[s, me], gs.at[s, j], gr.at[s, me], plane_dev(j))

    def gradient(s, lhs):
        def pair(j2):
            k = kt[s, pl.ds(j2 * 2, 2)].reshape(256, 2048)
            g = lax.dot_general(lhs, k, NT, preferred_element_type=F32).astype(BF16)
            gsend[s, j2 * 2] = g[:, 0:128]
            gsend[s, j2 * 2 + 1] = g[:, 128:256]

        def body(k, carry):
            j2 = lax.rem(me // 2 + k, 8)
            pair(j2)
            g_copy(s, j2 * 2).start()
            g_copy(s, j2 * 2 + 1).start()
            return carry

        lax.fori_loop(1, 8, body, 0)
        pair(me // 2)
        g_copy(s, me + 1 - 2 * lax.rem(me, 2)).start()

    def d_copy(s, j):
        return remote(dlow.at[s, me], dlow.at[s, me], ds_.at[s, j], dr.at[s, me], plane_dev(j))

    def f_copy(s, k):
        return remote(dall.at[s, e], dall.at[s, e], fs.at[s, k], fr.at[s, e], ring_dev(k))

    def make_delta(s):
        def square(k, total):
            j = lax.rem(me + k, 16)
            remote(sqsend.at[s, j], sqrecv.at[s, j], ss.at[s, j], sr.at[s, j], plane_dev(j)).wait_recv()
            return total + sqrecv[s, j]

        lane = iota((16, 128), 1)
        coef = jnp.where(lane < 48, own_coef[s], peer_coef[s])
        col_square = lax.fori_loop(1, 16, square, sqsend[s, me])
        inverse = 1.0 / (col_square[0:1] + RIDGE)

        def body(k, total):
            j = lax.rem(me + k, 16)
            remote(gsend.at[s, j], grecv.at[s, j], gs.at[s, j], gr.at[s, j], plane_dev(j)).wait_recv()
            return total + grecv[s, j].astype(F32)

        total = lax.fori_loop(1, 16, body, gsend[s, me].astype(F32) - RIDGE * coef)
        delta = total * inverse
        dlow[s, me] = delta.astype(BF16)
        dall[s, e] = delta

        def push(k, carry):
            d_copy(s, lax.rem(me + k, 16)).start()
            return carry

        lax.fori_loop(1, 16, push, 0)

    def push_delta(s):
        def push_ring(k, carry):
            f_copy(s, lax.rem(e + k, 8)).start()
            return carry

        lax.fori_loop(1, 8, push_ring, 0)

    def wait_delta(s):
        def body(k, carry):
            j = lax.rem(me + k, 16)
            remote(dlow.at[s, j], dlow.at[s, j], ds_.at[s, j], dr.at[s, j], plane_dev(j)).wait_recv()
            return carry

        lax.fori_loop(1, 16, body, 0)
        return jnp.concatenate([dlow[s, j] for j in range(16)], axis=1)

    def p_copy(to):
        return remote(psend.at[to], precv.at[e], ps.at[to], pr.at[e], ring_dev(to))

    def change(d):
        def chunk(to):
            rel = lax.rem(to // 4 + xl, 2) * 4 + lax.rem(to, 4)
            k = kt[0, :, :, pl.ds(pl.multiple_of(rel * 256, 256), 256)].reshape(2048, 256)
            psend[to] = jnp.dot(d, k, preferred_element_type=F32).astype(BF16)

        def body(k, carry):
            to = lax.rem(e + k, 8)
            chunk(to)
            p_copy(to).start()
            return carry

        lax.fori_loop(1, 8, body, 0)
        chunk(e)

    def sum_change():
        def body(k, total):
            j = lax.rem(e + k, 8)
            remote(psend.at[j], precv.at[j], ps.at[j], pr.at[j], ring_dev(j)).wait_recv()
            return total + precv[j].astype(F32)

        return lax.fori_loop(1, 8, body, psend[e].astype(F32))

    def update_coefs(s, base):
        def body(k, carry):
            j = lax.rem(e + k, 8)
            remote(dall.at[s, j], dall.at[s, j], fs.at[s, j], fr.at[s, j], ring_dev(j)).wait_recv()
            return carry

        lax.fori_loop(1, 8, body, 0)
        lane = iota((16, 128), 1)
        pieces, cols = [], []
        for k in range(4):
            own = dall[s, xl * 4 + k]
            other = dall[s, (1 - xl) * 4 + k]
            pieces.append(jnp.where(lane < 48, own, other))
            cols.append(jnp.broadcast_to(places[k, s, 0:1], (128, 128)).T)
        lhs = split3(jnp.concatenate(pieces, axis=1))
        col = jnp.concatenate(cols, axis=0)

        def step(k, carry):
            at = pl.ds(pl.multiple_of(k * 512, 512), 512)
            base_lane = (k * 512).astype(F32)
            hot = []
            for i in range(4):
                lanes = iota((512, 128), 1).astype(F32) + (base_lane + i * 128.0)
                hot.append((col == lanes).astype(F32).astype(BF16))
            three = jnp.dot(lhs, jnp.concatenate(hot, axis=1), preferred_element_type=F32)
            coef_out[:, at] = base[:, at] + sum3(three)
            return carry

        lax.fori_loop(0, 8, step, 0)

    for s in range(2):
        for j in range(16):
            kt[s, j, 96:128, :] = jnp.zeros((32, 2048), BF16)
    level(0, 1)
    level(0, 2)
    launch(1, 0)
    half_copy(1).wait_recv()
    launch(1, 1)
    tiles(0, 0, 0, 1)
    level(0, 3)
    for i in range(2):
        x_samples[i].wait_recv()
        hand[i].start()
    tiles(0, 0, 1, 3)
    level(0, 4)
    level(1, 1)
    tiles(0, 0, 3, 4)
    x_rows[0].wait_recv()
    x_rows[1].wait_recv()
    weight_rows(1)
    wt[:, 1024:2048] = peer_wt[...]
    for i in range(2):
        hand_in[i].wait_recv()
    tiles(0, 1, 0, 4)
    push_squares(0)
    level(1, 2)
    gradient(0, wt[...])
    tiles(1, 0, 0, 1)
    level(1, 3)
    tiles(1, 0, 1, 3)
    x_coef.wait_recv()
    make_delta(0)
    push_delta(0)
    level(1, 4)
    tiles(1, 0, 3, 4)
    tiles(1, 1, 0, 2)
    change(wait_delta(0))
    tiles(1, 1, 2, 3)
    chunk_at = pl.ds(pl.multiple_of(c * 256, 256), 256)
    pred = preds[:, chunk_at] + sum_change()

    def rel_to(to):
        return lax.rem(to // 4 + xl, 2) * 4 + c

    def w_copy(to):
        return remote(wt2.at[c], wt2.at[rel_to(to)], ws.at[to], wr.at[rel_to(to)], ring_dev(to))

    wt2[c] = (weights[:, chunk_at] * (targets[:, chunk_at] - pred)).astype(BF16)

    def push_w(k, carry):
        w_copy(lax.rem(e + k, 8)).start()
        return carry

    lax.fori_loop(1, 8, push_w, 0)
    pmid[c] = pred

    def q_copy(k):
        to = lax.rem(c + k, 4)
        return remote(pmid.at[c], pmid.at[c], qs.at[to], qr.at[c], (r, to))

    def push_q(k, carry):
        q_copy(k).start()
        return carry

    tiles(1, 1, 3, 4)
    push_squares(1)

    def wait_w(k, carry):
        j = lax.rem(c + k, 8)
        remote(wt2.at[j], wt2.at[j], ws.at[j], wr.at[j], ring_dev(j)).wait_recv()
        return carry

    lax.fori_loop(1, 8, wait_w, 0)
    gradient(1, jnp.concatenate([wt2[j] for j in range(8)], axis=1))
    lax.fori_loop(1, 4, push_q, 0)

    def wait_place(k, carry):
        j = lax.rem(c + k, 4)
        remote(place, places.at[j], ls.at[k], lr.at[j], (r, j)).wait_recv()
        return carry

    lax.fori_loop(1, 4, wait_place, 0)
    update_coefs(0, coefs)
    make_delta(1)
    push_delta(1)
    d = wait_delta(1)

    def e_copy(rel, half, across_x):
        to_xl = xl if rel == 0 else 1 - xl
        to_hi = c // 2 if across_x == 0 else 1 - c // 2
        n = (rel * 2 + half) * 2 + across_x
        dev = (to_xl * 16 + me, to_hi * 2 + half)
        return remote(lsend.at[rel * 2 + half], lrecv.at[e], es.at[n], er.at[e], dev)

    for rel in (1, 0):
        for half in range(2):
            k = kt[1, :, :, rel * 1024 + half * 512 : rel * 1024 + half * 512 + 512].reshape(2048, 512)
            lsend[rel * 2 + half] = jnp.dot(d, k, preferred_element_type=F32).astype(BF16)
            e_copy(rel, half, 1).start()
            if rel == 1:
                e_copy(rel, half, 0).start()
            else:
                pl.when(core != half)(lambda half=half: e_copy(0, half, 0).start())
    lrecv[e] = lsend[core]
    update_coefs(1, coef_out)

    def wait_q(k, carry):
        j = lax.rem(c + k, 4)
        remote(pmid.at[j], pmid.at[j], qs.at[j], qr.at[j], (r, j)).wait_recv()
        return carry

    lax.fori_loop(1, 4, wait_q, 0)

    def wait_e(k, carry):
        j = lax.rem(e + k, 8)
        remote(lrecv.at[j], lrecv.at[j], es.at[0], er.at[j], ring_dev(j)).wait_recv()
        return carry

    lax.fori_loop(1, 8, wait_e, 0)
    total = lrecv[0].astype(F32)
    for j in range(1, 8):
        total = total + lrecv[j].astype(F32)
    pend[core] = jnp.concatenate([pmid[core * 2], pmid[core * 2 + 1]], axis=1) + total
    final = remote(pend.at[core], pend.at[core], hs.at[2], hr.at[2], sibling)
    final.start()
    remote(pend.at[1 - core], pend.at[1 - core], hs.at[2], hr.at[2], sibling).wait_recv()
    pred_out[:, 0:512] = pend[0]
    pred_out[:, 512:1024] = pend[1]

    for s in range(2):
        half_copy(s).wait_send()
        for cp in started[s]:
            cp.wait_send()
    for cp in (*x_samples, *x_rows, x_coef, *hand, final):
        cp.wait_send()

    def drain_plane(k, carry):
        j = lax.rem(me + k, 16)
        for s in range(2):
            g_copy(s, j).wait_send()
            s_copy(s, j).wait_send()
            d_copy(s, j).wait_send()
        return carry

    def drain_ring(k, carry):
        j = lax.rem(e + k, 8)
        for s in range(2):
            f_copy(s, j).wait_send()
        p_copy(j).wait_send()
        w_copy(j).wait_send()
        return carry

    def drain_cent(k, carry):
        q_copy(k).wait_send()
        l_copy(k).wait_send()
        return carry

    lax.fori_loop(1, 16, drain_plane, 0)
    lax.fori_loop(1, 8, drain_ring, 0)
    lax.fori_loop(1, 4, drain_cent, 0)
    for rel in range(2):
        for half in range(2):
            e_copy(rel, half, 1).wait_send()
            if rel == 1:
                e_copy(rel, half, 0).wait_send()
            else:
                pl.when(core != half)(lambda half=half: e_copy(0, half, 0).wait_send())


def local(samples, weights, targets, predictions, centres, coefs, block_index):
    rows, depth = samples.shape
    pool = centres.shape[0]
    t = targets.shape[0]
    sharpness = 1.3 / math.sqrt(8.0 * depth)
    offset = 2.0 * depth * sharpness - 1.5 - 0.5 * math.log(rows * lax.axis_size("rows"))
    scale = sharpness * LOG2E
    shift = offset * LOG2E
    vmem = pl.BlockSpec(memory_space=pltpu.VMEM)
    hbm = pl.BlockSpec(memory_space=pl.ANY)
    sds = jax.ShapeDtypeStruct
    dma = pltpu.SemaphoreType.DMA
    pred, coef = pl.pallas_call(
        functools.partial(main_kernel, scale, shift),
        out_shape=(sds((t, rows), F32), sds((t, pool), F32)),
        in_specs=[hbm] * 7,
        out_specs=(vmem,) * 2,
        scratch_shapes=[
            pltpu.VMEM(block_index.shape, jnp.int32),
            pltpu.VMEM(centres.shape, BF16),
            pltpu.VMEM(coefs.shape, F32),
            pltpu.VMEM(samples.shape, BF16),
            pltpu.VMEM((1, rows), F32),
            pltpu.VMEM((t, rows), F32),
            pltpu.VMEM((t, rows), F32),
            pltpu.VMEM((256, pool), BF16),
            pltpu.VMEM((2, 48, depth), BF16),
            pltpu.VMEM((2, t, 128), F32),
            pltpu.VMEM((2, 8, 128), F32),
            pltpu.VMEM((t, rows), BF16),
            pltpu.VMEM((depth, rows), BF16),
            pltpu.VMEM((2, 16, 96, depth), BF16),
            pltpu.VMEM((depth, rows), BF16),
            pltpu.VMEM((2, t, 128), F32),
            pltpu.VMEM((4, 2, 8, 128), F32),
            pltpu.VMEM((t, 2 * rows), BF16),
            pltpu.VMEM((t, rows), BF16),
            pltpu.VMEM((2, 8, rows), F32),
            pltpu.VMEM((16, 2 * rows), BF16),
            pltpu.VMEM((2, 16, 128, 2 * rows), BF16),
            pltpu.VMEM((2, 16, t, 128), BF16),
            pltpu.VMEM((2, 16, t, 128), BF16),
            pltpu.VMEM((2, 16, 8, 128), F32),
            pltpu.VMEM((2, 16, 8, 128), F32),
            pltpu.VMEM((2, 16, t, 128), BF16),
            pltpu.VMEM((2, 8, t, 128), F32),
            pltpu.VMEM((8, t, 256), BF16),
            pltpu.VMEM((8, t, 256), BF16),
            pltpu.VMEM((4, t, 512), BF16),
            pltpu.VMEM((8, t, 512), BF16),
            pltpu.VMEM((8, t, 256), BF16),
            pltpu.VMEM((4, t, 256), F32),
            pltpu.VMEM((2, t, 512), F32),
            dma((7,)),
            dma((7,)), dma((7,)),
            dma((2, 30)), dma((2, 2, 16)),
            dma((2, 16)), dma((2, 16)),
            dma((2, 16)), dma((2, 16)),
            dma((2, 16)), dma((2, 16)),
            dma((2, 8)), dma((2, 8)),
            dma((8,)), dma((8,)),
            dma((8,)), dma((8,)),
            dma((8,)), dma((8,)),
            dma((4,)), dma((4,)),
            dma((4,)), dma((4,)),
            dma((3,)), dma((3,)),
        ],
        compiler_params=pltpu.CompilerParams(
            collective_id=0, has_side_effects=True, vmem_limit_bytes=60 * 2**20
        ),
    )(block_index, centres, coefs, samples, weights[None, :], targets, predictions)
    return coef, pred


def solution(mesh):
    in_specs = (
        P("rows", None),
        P("rows"),
        P(None, "rows"),
        P(None, "rows"),
        P("rows", None),
        P(None, "rows"),
        P(None, "cent"),
    )
    out_specs = (P(None, "rows"), P(None, "rows"))
    return jax.shard_map(local, mesh=mesh, in_specs=in_specs, out_specs=out_specs, check_vma=False)
```

```python
import functools
import math

import jax
import jax.numpy as jnp
from jax import lax
from jax.experimental import pallas as pl
from jax.experimental.pallas import tpu as pltpu
from jax.sharding import PartitionSpec as P

RIDGE = 1.0
MESH = pl.DeviceIdType.MESH
F32, BF16 = jnp.float32, jnp.bfloat16
LOG2E = 1.4426950408889634
NT = (((1,), (1,)), ((), ()))


def iota(shape, axis):
    return lax.broadcasted_iota(jnp.int32, shape, axis)


def split3(v):
    hi = v.astype(BF16)
    rest = v - hi.astype(F32)
    mid = rest.astype(BF16)
    low = (rest - mid.astype(F32)).astype(BF16)
    return jnp.concatenate([hi, mid, low], axis=0)


def sum3(v):
    return v[0:16] + v[16:32] + v[32:48]


def main_kernel(scale, shift, blk_in, centres_in, coefs_in, samples_in, weights_in, targets_in, preds_in,
                pred_hbm, coef_hbm, pred_out, coef_out,
                blk, centres, coefs, samples, weights, targets, preds, select,
                outgoing, own_coef, place, weighted, samples_t,
                cent, peer_t, peer_coef, places, wt, peer_wt, auxes, wcat, kt, gsend, grecv, sqsend, sqrecv,
                dlow, dall, psend, precv, lsend, lrecv, wt2, pmid, pend,
                loads, xs, xr, cs, cr, gs, gr, ss, sr, ds_, dr, fs, fr, ps, pr, es, er, ws, wr, qs, qr, ls, lr,
                hs, hr):
    r = lax.axis_index("rows")
    c = lax.axis_index("cent")
    xl = r // 16
    me = lax.rem(r, 16)
    z = me // 4
    y = lax.rem(me, 4)
    e = xl * 4 + c
    core = lax.rem(c, 2)

    def wrap(v):
        return lax.rem(v + 8, 4)

    def offset_of(i):
        return 2 - i + 3 * (i // 2) - 2 * (i // 3)

    def peer_of(k):
        return wrap(z + offset_of(k // 4)) * 4 + wrap(y + offset_of(lax.rem(k, 4)))

    def ring_of(k):
        m = k + 2 - 7 * (k // 6) - 2 * (k // 7)
        hi = lax.rem(c // 2 + m // 2, 2)
        return lax.rem(xl + m // 4, 2) * 4 + hi * 2 + lax.rem(c + m, 2)

    def plane_dev(j):
        return (xl * 16 + j, c)

    def ring_dev(k):
        return ((k // 4) * 16 + me, lax.rem(k, 4))

    pairs = ((blk_in, blk), (centres_in, centres), (samples_in, samples), (coefs_in, coefs),
             (weights_in, weights), (targets_in, targets), (preds_in, preds))
    fetch = [pltpu.make_async_copy(src, dst, loads.at[i]) for i, (src, dst) in enumerate(pairs)]
    for cp in fetch:
        cp.start()

    barrier = pltpu.get_barrier_semaphore()

    neighbours = (
        plane_dev(z * 4 + wrap(y + 1)),
        plane_dev(z * 4 + wrap(y - 1)),
        plane_dev(wrap(z + 1) * 4 + y),
        plane_dev(wrap(z - 1) * 4 + y),
        ((1 - xl) * 16 + me, c),
        ((1 - xl) * 16 + me, lax.rem(c + 2, 4)),
        (r, c + 1 - 2 * core),
    )
    for dev in neighbours:
        pl.semaphore_signal(barrier, inc=1, device_id=dev, device_id_type=MESH)

    pool = centres.shape[0]
    q_rows = blk.shape[1] // 128
    upper = (iota((128, 128), 0) <= iota((128, 128), 1)).astype(F32)
    lower = (iota((q_rows, q_rows), 0) > iota((q_rows, q_rows), 1)).astype(F32)
    rank_of = iota((128, 128), 0).astype(F32)
    fetch[0].wait()
    for s in range(2):
        index = jnp.concatenate([blk[s : s + 1, q * 128 : (q + 1) * 128] for q in range(q_rows)], axis=0)
        at = index - r * pool
        mine = jnp.logical_and(at >= 0, at < pool)
        flag = mine.astype(F32)
        inner = jnp.dot(flag, upper, preferred_element_type=F32)
        before = jnp.sum(jnp.dot(lower, flag, preferred_element_type=F32), axis=1, keepdims=True)
        rank = jnp.where(mine, inner + before - 1.0, -1.0)
        at_f = at.astype(F32)
        acc = jnp.zeros((128, 128), F32)
        for q in range(q_rows):
            acc = acc + jnp.where(rank[q : q + 1, :] == rank_of, at_f[q : q + 1, :], 0.0)
        col = jnp.where(iota((128, 1), 0) < 96, jnp.sum(acc, axis=1, keepdims=True), -1.0)
        row = jnp.where(iota((1, 128), 1) < 96, jnp.sum(acc.T, axis=0, keepdims=True), -1.0)
        place[s] = jnp.broadcast_to(row, (8, 128))
        for k in range(0, pool, 512):
            lanes = (iota((128, 512), 1) + k).astype(F32)
            select[s * 128 : (s + 1) * 128, k : k + 512] = (col == lanes).astype(F32).astype(BF16)
    fetch[1].wait()
    rows = jnp.dot(select[...], centres[...], preferred_element_type=F32).astype(BF16)
    for s in range(2):
        cent[s, me, 0:48] = rows[s * 128 : s * 128 + 48]
        outgoing[s] = rows[s * 128 + 48 : s * 128 + 96]
    fetch[2].wait()
    samples_t[...] = samples[...].T

    pl.semaphore_wait(barrier, len(neighbours))

    def remote(src, dst, ssem, rsem, dev):
        return pltpu.make_async_remote_copy(src_ref=src, dst_ref=dst, send_sem=ssem, recv_sem=rsem,
                                            device_id=dev, device_id_type=MESH)

    partner = ((1 - xl) * 16 + me, c)
    across = ((1 - xl) * 16 + me, lax.rem(c + 2, 4))
    sibling = (r, c + 1 - 2 * core)

    def half_copy(s):
        return remote(outgoing.at[s], cent.at[s, me, pl.ds(48, 48)], xs.at[s], xr.at[s], partner)

    counters = [0, 0]
    started = [[], []]

    def slot(part, a, b):
        if part == 0:
            return wrap(z + b) * 4 + wrap(y + a)
        return wrap(z + a) * 4 + wrap(y + b)

    def send(s, part, j, a, b):
        n = counters[s]
        counters[s] += 1
        ref = cent.at[s, j, pl.ds(48 * part, 48)]
        cp = remote(ref, ref, cs.at[s, n], cr.at[s, part, j], plane_dev(slot(part, a, b)))
        cp.start()
        started[s].append(cp)

    def got(s, part, j):
        ref = cent.at[s, j, pl.ds(48 * part, 48)]
        remote(ref, ref, cs.at[s, 0], cr.at[s, part, j], plane_dev(slot(part, 1, 0))).wait_recv()

    def launch(s, part):
        for a, b in ((1, 0), (-1, 0), (0, 1), (0, -1)):
            send(s, part, me, a, b)

    def near(s, part, sign):
        j = slot(part, -sign, 0)
        got(s, part, j)
        if (sign == 1) == (s == part):
            send(s, part, j, sign, 0)
        send(s, part, j, 0, 1)
        send(s, part, j, 0, -1)

    def far(s, part):
        j = slot(part, 2, 0)
        got(s, part, j)
        send(s, part, j, 0, 1)
        send(s, part, j, 0, -1)

    def second(s, part, d, sign):
        j = slot(part, d, -sign)
        got(s, part, j)
        if (sign == 1) == (d in (0, -1)):
            send(s, part, j, 0, sign)

    def last(s, part, d):
        got(s, part, slot(part, d, 2))

    def level(s, part, n):
        if n == 1:
            near(s, part, 1)
            near(s, part, -1)
            second(s, part, 0, 1)
            second(s, part, 0, -1)
        elif n == 2:
            far(s, part)
            for d in (1, -1):
                second(s, part, d, 1)
                second(s, part, d, -1)
            last(s, part, 0)
        elif n == 3:
            second(s, part, 2, 1)
            second(s, part, 2, -1)
            last(s, part, 1)
            last(s, part, -1)
        else:
            last(s, part, 2)

    half_copy(0).start()
    launch(0, 0)
    half_copy(1).start()

    cut = 112
    depth = samples_t.shape[0]
    low_f = pl.ds(pl.multiple_of(core * 256, 16), cut)
    high_f = pl.ds(pl.multiple_of(core * 256 + cut, 16), 256 - cut)
    sib_low = pl.ds(pl.multiple_of((1 - core) * 256, 16), cut)
    sib_high = pl.ds(pl.multiple_of((1 - core) * 256 + cut, 16), 256 - cut)
    x_samples = [
        remote(samples_t.at[low_f], peer_t.at[low_f], xs.at[2], xr.at[2], partner),
        remote(samples_t.at[high_f], peer_t.at[high_f], xs.at[3], xr.at[3], across),
    ]
    for cp in x_samples:
        cp.start()
    hand = [
        remote(peer_t.at[low_f], peer_t.at[low_f], hs.at[0], hr.at[0], sibling),
        remote(peer_t.at[high_f], peer_t.at[high_f], hs.at[1], hr.at[1], sibling),
    ]
    hand_in = [
        remote(peer_t.at[sib_low], peer_t.at[sib_low], hs.at[0], hr.at[0], sibling),
        remote(peer_t.at[sib_high], peer_t.at[sib_high], hs.at[1], hr.at[1], sibling),
    ]

    for i in (4, 5, 6):
        fetch[i].wait()
    xf = samples[...].astype(F32)
    sq = xf * xf
    sq_hi = sq.astype(BF16)
    sq_lo = (sq - sq_hi.astype(F32)).astype(BF16)
    ones = jnp.ones((16, depth), BF16)
    norm = (lax.dot_general(ones, sq_hi, NT, preferred_element_type=F32)
            + lax.dot_general(ones, sq_lo, NT, preferred_element_type=F32))
    w = weights[...]
    auxes[0] = jnp.where(iota((8, 1024), 0) == 0, w, -scale * norm[0:8])
    weighted[...] = (w * (targets[...] - preds[...])).astype(BF16)
    wt[:, 0:1024] = weighted[...]

    def weight_rows(half):
        v = auxes[half, 0:1]
        hi = v.astype(BF16).astype(F32)
        which = iota((16, 1024), 0)
        full = jnp.where(which == 0, hi, jnp.where(which == 1, v - hi, 0.0))
        wcat[:, half * 1024 : (half + 1) * 1024] = full.astype(BF16)

    weight_rows(0)
    x_rows = [
        remote(auxes.at[0], auxes.at[1], xs.at[4], xr.at[4], partner),
        remote(weighted, peer_wt, xs.at[5], xr.at[5], partner),
    ]
    for cp in x_rows:
        cp.start()

    half_copy(0).wait_recv()
    launch(0, 1)

    fetch[3].wait()
    parts = split3(coefs[...])
    for s in range(2):
        own_coef[s] = sum3(lax.dot_general(parts, select[s * 128 : (s + 1) * 128, :], NT,
                                           preferred_element_type=F32))
    x_coef = remote(own_coef, peer_coef, xs.at[6], xr.at[6], partner)
    x_coef.start()

    def l_copy(k):
        return remote(place, places.at[c], ls.at[k], lr.at[c], (r, lax.rem(c + k, 4)))

    def share_place(k, carry):
        l_copy(k).start()
        return carry

    places[c] = place[...]

    def tiles(s, half, first, stop):
        src = samples_t if half == 0 else peer_t
        base = half * 1024

        def body(k, carry):
            g = lax.rem(z + k + k // 2 - 2 * (k // 3), 4)
            picked = cent[s, pl.ds(g * 4, 4)].reshape(384, 512)
            wide = picked.astype(F32)
            a = shift - scale * jnp.sum(wide * wide, axis=1, keepdims=True)
            for i in range(4):
                prod = jnp.dot(picked, src[:, i * 256 : (i + 1) * 256], preferred_element_type=F32)
                b = auxes[half, 1:2, i * 256 : (i + 1) * 256]
                val = jnp.exp2(prod * (2.0 * scale) + (a + b)).astype(BF16)
                lo = base + i * 256
                for q in range(4):
                    kt[s, g * 4 + q, 0:96, lo : lo + 256] = val[q * 96 : (q + 1) * 96]
            for q in (0, 2):
                k2 = kt[s, pl.ds(g * 4 + q, 2), :, base : base + 1024].reshape(256, 1024)
                part = lax.dot_general(wcat[:, base : base + 1024], k2 * k2, NT, preferred_element_type=F32)
                tot = jnp.broadcast_to(part[0:1] + part[1:2], (8, 256))
                for h in range(2):
                    now = tot[:, h * 128 : (h + 1) * 128]
                    if half == 0:
                        sqsend[s, g * 4 + q + h] = now
                    else:
                        sqsend[s, g * 4 + q + h] += now
            return carry

        lax.fori_loop(first, stop, body, 0)

    def s_copy(s, j):
        return remote(sqsend.at[s, j], sqrecv.at[s, me], ss.at[s, j], sr.at[s, me], plane_dev(j))

    def push_squares(s):
        def body(k, carry):
            s_copy(s, lax.rem(me + k, 16)).start()
            return carry

        lax.fori_loop(1, 16, body, 0)

    def g_copy(s, j):
        return remote(gsend.at[s, j], grecv.at[s, me], gs.at[s, j], gr.at[s, me], plane_dev(j))

    def gradient(s, lhs):
        def pair(j2):
            k = kt[s, pl.ds(j2 * 2, 2)].reshape(256, 2048)
            g = lax.dot_general(lhs, k, NT, preferred_element_type=F32).astype(BF16)
            gsend[s, j2 * 2] = g[:, 0:128]
            gsend[s, j2 * 2 + 1] = g[:, 128:256]

        def body(k, carry):
            j2 = wrap(z + offset_of(k // 2)) * 2 + lax.rem(y // 2 + 1 + k, 2)
            pair(j2)
            g_copy(s, j2 * 2).start()
            g_copy(s, j2 * 2 + 1).start()
            return carry

        lax.fori_loop(0, 7, body, 0)
        pair(me // 2)
        g_copy(s, me + 1 - 2 * lax.rem(me, 2)).start()

    def d_copy(s, j):
        return remote(dlow.at[s, me], dlow.at[s, me], ds_.at[s, j], dr.at[s, me], plane_dev(j))

    def f_copy(s, k):
        return remote(dall.at[s, e], dall.at[s, e], fs.at[s, k], fr.at[s, e], ring_dev(k))

    def make_delta(s):
        def square(k, total):
            j = lax.rem(me + k, 16)
            remote(sqsend.at[s, j], sqrecv.at[s, j], ss.at[s, j], sr.at[s, j], plane_dev(j)).wait_recv()
            return total + sqrecv[s, j]

        lane = iota((16, 128), 1)
        coef = jnp.where(lane < 48, own_coef[s], peer_coef[s])
        col_square = lax.fori_loop(1, 16, square, sqsend[s, me])
        inverse = 1.0 / (col_square[0:1] + RIDGE)

        def body(k, total):
            j = lax.rem(me + k, 16)
            remote(gsend.at[s, j], grecv.at[s, j], gs.at[s, j], gr.at[s, j], plane_dev(j)).wait_recv()
            return total + grecv[s, j].astype(F32)

        total = lax.fori_loop(1, 16, body, gsend[s, me].astype(F32) - RIDGE * coef)
        delta = total * inverse
        dlow[s, me] = delta.astype(BF16)
        dall[s, e] = delta

        def push(k, carry):
            d_copy(s, peer_of(k)).start()
            return carry

        lax.fori_loop(0, 15, push, 0)

    def push_delta(s):
        def push_ring(k, carry):
            f_copy(s, lax.rem(e + k, 8)).start()
            return carry

        lax.fori_loop(1, 8, push_ring, 0)

    def wait_delta(s):
        def body(k, carry):
            j = lax.rem(me + k, 16)
            remote(dlow.at[s, j], dlow.at[s, j], ds_.at[s, j], dr.at[s, j], plane_dev(j)).wait_recv()
            return carry

        lax.fori_loop(1, 16, body, 0)
        return jnp.concatenate([dlow[s, j] for j in range(16)], axis=1)

    def p_copy(to):
        return remote(psend.at[to], precv.at[e], ps.at[to], pr.at[e], ring_dev(to))

    def change(d):
        def chunk(to):
            rel = lax.rem(to // 4 + xl, 2) * 4 + lax.rem(to, 4)
            k = kt[0, :, :, pl.ds(pl.multiple_of(rel * 256, 256), 256)].reshape(2048, 256)
            psend[to] = jnp.dot(d, k, preferred_element_type=F32).astype(BF16)

        def body(k, carry):
            to = ring_of(k)
            chunk(to)
            p_copy(to).start()
            return carry

        lax.fori_loop(0, 7, body, 0)
        chunk(e)

    def sum_change():
        def body(k, total):
            j = lax.rem(e + k, 8)
            remote(psend.at[j], precv.at[j], ps.at[j], pr.at[j], ring_dev(j)).wait_recv()
            return total + precv[j].astype(F32)

        return lax.fori_loop(1, 8, body, psend[e].astype(F32))

    def update_coefs(s, base):
        def body(k, carry):
            j = lax.rem(e + k, 8)
            remote(dall.at[s, j], dall.at[s, j], fs.at[s, j], fr.at[s, j], ring_dev(j)).wait_recv()
            return carry

        lax.fori_loop(1, 8, body, 0)
        lane = iota((16, 128), 1)
        pieces, cols = [], []
        for k in range(4):
            own = dall[s, xl * 4 + k]
            other = dall[s, (1 - xl) * 4 + k]
            pieces.append(jnp.where(lane < 48, own, other))
            cols.append(jnp.broadcast_to(places[k, s, 0:1], (128, 128)).T)
        lhs = split3(jnp.concatenate(pieces, axis=1))
        col = jnp.concatenate(cols, axis=0)

        def step(k, carry):
            at = pl.ds(pl.multiple_of(k * 512, 512), 512)
            base_lane = (k * 512).astype(F32)
            hot = []
            for i in range(4):
                lanes = iota((512, 128), 1).astype(F32) + (base_lane + i * 128.0)
                hot.append((col == lanes).astype(F32).astype(BF16))
            three = jnp.dot(lhs, jnp.concatenate(hot, axis=1), preferred_element_type=F32)
            coef_out[:, at] = base[:, at] + sum3(three)
            return carry

        lax.fori_loop(0, 8, step, 0)

    level(0, 0, 1)
    for s in range(2):
        for j in range(16):
            kt[s, j, 96:128, :] = jnp.zeros((32, 2048), BF16)
    level(0, 0, 2)
    level(0, 1, 1)
    level(0, 0, 3)
    level(0, 1, 2)
    tiles(0, 0, 0, 1)
    launch(1, 0)
    half_copy(1).wait_recv()
    launch(1, 1)
    level(0, 0, 4)
    level(0, 1, 3)
    for i in range(2):
        x_samples[i].wait_recv()
        hand[i].start()
    tiles(0, 0, 1, 3)
    level(1, 0, 1)
    level(1, 1, 1)
    x_rows[0].wait_recv()
    x_rows[1].wait_recv()
    weight_rows(1)
    wt[:, 1024:2048] = peer_wt[...]
    for i in range(2):
        hand_in[i].wait_recv()
    lax.fori_loop(1, 4, share_place, 0)
    tiles(0, 1, 0, 3)
    level(0, 1, 4)
    tiles(0, 0, 3, 4)
    tiles(0, 1, 3, 4)
    push_squares(0)
    gradient(0, wt[...])
    level(1, 0, 2)
    level(1, 1, 2)
    tiles(1, 0, 0, 1)
    tiles(1, 1, 0, 1)
    x_coef.wait_recv()
    make_delta(0)
    level(1, 0, 3)
    level(1, 1, 3)
    push_delta(0)
    tiles(1, 0, 1, 3)
    tiles(1, 1, 1, 2)
    change(wait_delta(0))
    level(1, 0, 4)
    level(1, 1, 4)
    tiles(1, 1, 2, 3)
    tiles(1, 0, 3, 4)
    chunk_at = pl.ds(pl.multiple_of(c * 256, 256), 256)
    pred = preds[:, chunk_at] + sum_change()

    def rel_to(to):
        return lax.rem(to // 4 + xl, 2) * 4 + c

    def w_copy(to):
        return remote(wt2.at[c], wt2.at[rel_to(to)], ws.at[to], wr.at[rel_to(to)], ring_dev(to))

    wt2[c] = (weights[:, chunk_at] * (targets[:, chunk_at] - pred)).astype(BF16)

    def push_w(k, carry):
        w_copy(ring_of(k)).start()
        return carry

    lax.fori_loop(0, 7, push_w, 0)
    pmid[c] = pred

    def q_copy(k):
        to = lax.rem(c + k, 4)
        return remote(pmid.at[c], pmid.at[c], qs.at[to], qr.at[c], (r, to))

    def push_q(k, carry):
        q_copy(k).start()
        return carry

    tiles(1, 1, 3, 4)
    push_squares(1)

    def wait_w(k, carry):
        j = lax.rem(c + k, 8)
        remote(wt2.at[j], wt2.at[j], ws.at[j], wr.at[j], ring_dev(j)).wait_recv()
        return carry

    lax.fori_loop(1, 8, wait_w, 0)
    gradient(1, jnp.concatenate([wt2[j] for j in range(8)], axis=1))
    lax.fori_loop(1, 4, push_q, 0)

    def wait_place(k, carry):
        j = lax.rem(c + k, 4)
        remote(place, places.at[j], ls.at[k], lr.at[j], (r, j)).wait_recv()
        return carry

    lax.fori_loop(1, 4, wait_place, 0)
    update_coefs(0, coefs)
    make_delta(1)
    push_delta(1)
    d = wait_delta(1)

    def e_copy(rel, half, across_x):
        to_xl = xl if rel == 0 else 1 - xl
        to_hi = c // 2 if across_x == 0 else 1 - c // 2
        n = (rel * 2 + half) * 2 + across_x
        dev = (to_xl * 16 + me, to_hi * 2 + half)
        return remote(lsend.at[rel * 2 + half], lrecv.at[e], es.at[n], er.at[e], dev)

    for rel in range(2):
        for half in range(2):
            k = kt[1, :, :, rel * 1024 + half * 512 : rel * 1024 + half * 512 + 512].reshape(2048, 512)
            lsend[rel * 2 + half] = jnp.dot(d, k, preferred_element_type=F32).astype(BF16)
            e_copy(rel, half, 1).start()
            if rel == 1:
                e_copy(rel, half, 0).start()
            else:
                pl.when(core != half)(lambda half=half: e_copy(0, half, 0).start())
    lrecv[e] = lsend[core]
    update_coefs(1, coef_out)
    store_coef = pltpu.make_async_copy(coef_out, coef_hbm, loads.at[7])
    store_coef.start()

    def wait_q(k, carry):
        j = lax.rem(c + k, 4)
        remote(pmid.at[j], pmid.at[j], qs.at[j], qr.at[j], (r, j)).wait_recv()
        return carry

    lax.fori_loop(1, 4, wait_q, 0)

    def wait_e(k, carry):
        j = lax.rem(e + k, 8)
        remote(lrecv.at[j], lrecv.at[j], es.at[0], er.at[j], ring_dev(j)).wait_recv()
        return carry

    lax.fori_loop(1, 8, wait_e, 0)
    total = lrecv[0].astype(F32)
    for j in range(1, 8):
        total = total + lrecv[j].astype(F32)
    pend[core] = jnp.concatenate([pmid[core * 2], pmid[core * 2 + 1]], axis=1) + total
    final = remote(pend.at[core], pend.at[core], hs.at[2], hr.at[2], sibling)
    final.start()
    remote(pend.at[1 - core], pend.at[1 - core], hs.at[2], hr.at[2], sibling).wait_recv()
    pred_out[:, 0:512] = pend[0]
    pred_out[:, 512:1024] = pend[1]

    store_pred = pltpu.make_async_copy(pred_out, pred_hbm, loads.at[8])
    store_pred.start()
    for s in range(2):
        half_copy(s).wait_send()
        for cp in started[s]:
            cp.wait_send()
    for cp in (*x_samples, *x_rows, x_coef, *hand, final):
        cp.wait_send()

    def drain_plane(k, carry):
        j = lax.rem(me + k, 16)
        for s in range(2):
            g_copy(s, j).wait_send()
            s_copy(s, j).wait_send()
            d_copy(s, j).wait_send()
        return carry

    def drain_ring(k, carry):
        j = lax.rem(e + k, 8)
        for s in range(2):
            f_copy(s, j).wait_send()
        p_copy(j).wait_send()
        w_copy(j).wait_send()
        return carry

    def drain_cent(k, carry):
        q_copy(k).wait_send()
        l_copy(k).wait_send()
        return carry

    store_coef.wait()
    lax.fori_loop(1, 16, drain_plane, 0)
    lax.fori_loop(1, 8, drain_ring, 0)
    lax.fori_loop(1, 4, drain_cent, 0)
    for rel in range(2):
        for half in range(2):
            e_copy(rel, half, 1).wait_send()
            if rel == 1:
                e_copy(rel, half, 0).wait_send()
            else:
                pl.when(core != half)(lambda half=half: e_copy(0, half, 0).wait_send())
    store_pred.wait()


def local(samples, weights, targets, predictions, centres, coefs, block_index):
    rows, depth = samples.shape
    pool = centres.shape[0]
    t = targets.shape[0]
    sharpness = 1.3 / math.sqrt(8.0 * depth)
    offset = 2.0 * depth * sharpness - 1.5 - 0.5 * math.log(rows * lax.axis_size("rows"))
    scale = sharpness * LOG2E
    shift = offset * LOG2E
    vmem = pl.BlockSpec(memory_space=pltpu.VMEM)
    hbm = pl.BlockSpec(memory_space=pl.ANY)
    sds = jax.ShapeDtypeStruct
    dma = pltpu.SemaphoreType.DMA
    pred, coef = pl.pallas_call(
        functools.partial(main_kernel, scale, shift),
        out_shape=(sds((t, rows), F32), sds((t, pool), F32)),
        in_specs=[hbm] * 7,
        out_specs=(hbm,) * 2,
        scratch_shapes=[
            pltpu.VMEM((t, rows), F32),
            pltpu.VMEM((t, pool), F32),
            pltpu.VMEM(block_index.shape, jnp.int32),
            pltpu.VMEM(centres.shape, BF16),
            pltpu.VMEM(coefs.shape, F32),
            pltpu.VMEM(samples.shape, BF16),
            pltpu.VMEM((1, rows), F32),
            pltpu.VMEM((t, rows), F32),
            pltpu.VMEM((t, rows), F32),
            pltpu.VMEM((256, pool), BF16),
            pltpu.VMEM((2, 48, depth), BF16),
            pltpu.VMEM((2, t, 128), F32),
            pltpu.VMEM((2, 8, 128), F32),
            pltpu.VMEM((t, rows), BF16),
            pltpu.VMEM((depth, rows), BF16),
            pltpu.VMEM((2, 16, 96, depth), BF16),
            pltpu.VMEM((depth, rows), BF16),
            pltpu.VMEM((2, t, 128), F32),
            pltpu.VMEM((4, 2, 8, 128), F32),
            pltpu.VMEM((t, 2 * rows), BF16),
            pltpu.VMEM((t, rows), BF16),
            pltpu.VMEM((2, 8, rows), F32),
            pltpu.VMEM((16, 2 * rows), BF16),
            pltpu.VMEM((2, 16, 128, 2 * rows), BF16),
            pltpu.VMEM((2, 16, t, 128), BF16),
            pltpu.VMEM((2, 16, t, 128), BF16),
            pltpu.VMEM((2, 16, 8, 128), F32),
            pltpu.VMEM((2, 16, 8, 128), F32),
            pltpu.VMEM((2, 16, t, 128), BF16),
            pltpu.VMEM((2, 8, t, 128), F32),
            pltpu.VMEM((8, t, 256), BF16),
            pltpu.VMEM((8, t, 256), BF16),
            pltpu.VMEM((4, t, 512), BF16),
            pltpu.VMEM((8, t, 512), BF16),
            pltpu.VMEM((8, t, 256), BF16),
            pltpu.VMEM((4, t, 256), F32),
            pltpu.VMEM((2, t, 512), F32),
            dma((9,)),
            dma((7,)), dma((7,)),
            dma((2, 30)), dma((2, 2, 16)),
            dma((2, 16)), dma((2, 16)),
            dma((2, 16)), dma((2, 16)),
            dma((2, 16)), dma((2, 16)),
            dma((2, 8)), dma((2, 8)),
            dma((8,)), dma((8,)),
            dma((8,)), dma((8,)),
            dma((8,)), dma((8,)),
            dma((4,)), dma((4,)),
            dma((4,)), dma((4,)),
            dma((3,)), dma((3,)),
        ],
        compiler_params=pltpu.CompilerParams(
            collective_id=0, has_side_effects=True, vmem_limit_bytes=60 * 2**20
        ),
    )(block_index, centres, coefs, samples, weights[None, :], targets, predictions)
    return coef, pred


def solution(mesh):
    in_specs = (
        P("rows", None),
        P("rows"),
        P(None, "rows"),
        P(None, "rows"),
        P("rows", None),
        P(None, "rows"),
        P(None, "cent"),
    )
    out_specs = (P(None, "rows"), P(None, "rows"))
    return jax.shard_map(local, mesh=mesh, in_specs=in_specs, out_specs=out_specs, check_vma=False)
```

```python
import functools
import math

import jax
import jax.numpy as jnp
from jax import lax
from jax.experimental import pallas as pl
from jax.experimental.pallas import tpu as pltpu
from jax.sharding import PartitionSpec as P

RIDGE = 1.0
KEEP = 64
MESH = pl.DeviceIdType.MESH
F32, BF16 = jnp.float32, jnp.bfloat16
LOG2E = 1.4426950408889634
NT = (((1,), (1,)), ((), ()))


def iota(shape, axis):
    return lax.broadcasted_iota(jnp.int32, shape, axis)


def split3(v):
    hi = v.astype(BF16)
    rest = v - hi.astype(F32)
    mid = rest.astype(BF16)
    low = (rest - mid.astype(F32)).astype(BF16)
    return jnp.concatenate([hi, mid, low], axis=0)


def sum3(v):
    return v[0:16] + v[16:32] + v[32:48]


def main_kernel(scale, shift, blk_in, centres_in, coefs_in, samples_in, weights_in, targets_in, preds_in,
                pred_hbm, coef_hbm, pred_out, coef_out,
                blk, centres, coefs, samples, weights, targets, preds, select,
                outgoing, own_coef, place, weighted, samples_t,
                cent, peer_t, peer_coef, places, wt, peer_wt, auxes, wcat, kt, gsend, grecv, sqsend, sqrecv,
                dlow, dall, psend, precv, lsend, lrecv, wt2, pmid, pend,
                loads, xs, xr, cs, cr, gs, gr, ss, sr, ds_, dr, fs, fr, ps, pr, es, er, ws, wr, qs, qr, ls, lr,
                hs, hr):
    r = lax.axis_index("rows")
    c = lax.axis_index("cent")
    xl = r // 16
    me = lax.rem(r, 16)
    z = me // 4
    y = lax.rem(me, 4)
    e = xl * 4 + c
    core = lax.rem(c, 2)

    def wrap(v):
        return lax.rem(v + 8, 4)

    def offset_of(i):
        return 2 - i + 3 * (i // 2) - 2 * (i // 3)

    def peer_of(k):
        return wrap(z + offset_of(k // 4)) * 4 + wrap(y + offset_of(lax.rem(k, 4)))

    def ring_of(k):
        m = k + 2 - 7 * (k // 6) - 2 * (k // 7)
        hi = lax.rem(c // 2 + m // 2, 2)
        return lax.rem(xl + m // 4, 2) * 4 + hi * 2 + lax.rem(c + m, 2)

    def plane_dev(j):
        return (xl * 16 + j, c)

    def ring_dev(k):
        return ((k // 4) * 16 + me, lax.rem(k, 4))

    pairs = ((blk_in, blk), (centres_in, centres), (samples_in, samples), (coefs_in, coefs),
             (weights_in, weights), (targets_in, targets), (preds_in, preds))
    fetch = [pltpu.make_async_copy(src, dst, loads.at[i]) for i, (src, dst) in enumerate(pairs)]
    for cp in fetch:
        cp.start()

    barrier = pltpu.get_barrier_semaphore()

    neighbours = (
        plane_dev(z * 4 + wrap(y + 1)),
        plane_dev(z * 4 + wrap(y - 1)),
        plane_dev(wrap(z + 1) * 4 + y),
        plane_dev(wrap(z - 1) * 4 + y),
        ((1 - xl) * 16 + me, c),
        ((1 - xl) * 16 + me, lax.rem(c + 2, 4)),
        (r, c + 1 - 2 * core),
    )
    for dev in neighbours:
        pl.semaphore_signal(barrier, inc=1, device_id=dev, device_id_type=MESH)

    pool = centres.shape[0]
    q_rows = blk.shape[1] // 128
    upper = (iota((128, 128), 0) <= iota((128, 128), 1)).astype(F32)
    lower = (iota((q_rows, q_rows), 0) > iota((q_rows, q_rows), 1)).astype(F32)
    rank_of = iota((128, 128), 0).astype(F32)
    fetch[0].wait()
    for s in range(2):
        index = jnp.concatenate([blk[s : s + 1, q * 128 : (q + 1) * 128] for q in range(q_rows)], axis=0)
        at = index - r * pool
        mine = jnp.logical_and(at >= 0, at < pool)
        flag = mine.astype(F32)
        inner = jnp.dot(flag, upper, preferred_element_type=F32)
        before = jnp.sum(jnp.dot(lower, flag, preferred_element_type=F32), axis=1, keepdims=True)
        rank = jnp.where(mine, inner + before - 1.0, -1.0)
        at_f = at.astype(F32)
        acc = jnp.zeros((128, 128), F32)
        for q in range(q_rows):
            acc = acc + jnp.where(rank[q : q + 1, :] == rank_of, at_f[q : q + 1, :], 0.0)
        col = jnp.where(iota((128, 1), 0) < 96, jnp.sum(acc, axis=1, keepdims=True), -1.0)
        row = jnp.where(iota((1, 128), 1) < 96, jnp.sum(acc.T, axis=0, keepdims=True), -1.0)
        place[s] = jnp.broadcast_to(row, (8, 128))
        for k in range(0, pool, 512):
            lanes = (iota((128, 512), 1) + k).astype(F32)
            select[s * 128 : (s + 1) * 128, k : k + 512] = (col == lanes).astype(F32).astype(BF16)
    fetch[1].wait()
    rows = jnp.dot(select[...], centres[...], preferred_element_type=F32).astype(BF16)
    for s in range(2):
        cent[s, me, 0:KEEP] = rows[s * 128 : s * 128 + KEEP]
        outgoing[s] = rows[s * 128 + KEEP : s * 128 + 96]
    fetch[2].wait()
    samples_t[...] = samples[...].T

    pl.semaphore_wait(barrier, len(neighbours))

    def remote(src, dst, ssem, rsem, dev):
        return pltpu.make_async_remote_copy(src_ref=src, dst_ref=dst, send_sem=ssem, recv_sem=rsem,
                                            device_id=dev, device_id_type=MESH)

    partner = ((1 - xl) * 16 + me, c)
    across = ((1 - xl) * 16 + me, lax.rem(c + 2, 4))
    sibling = (r, c + 1 - 2 * core)

    def half_copy(s):
        return remote(outgoing.at[s], cent.at[s, me, pl.ds(KEEP, 96 - KEEP)], xs.at[s], xr.at[s], partner)

    counters = [0, 0]
    started = [[], []]

    def slot(part, a, b):
        if part == 0:
            return wrap(z + b) * 4 + wrap(y + a)
        return wrap(z + a) * 4 + wrap(y + b)

    def send(s, part, j, a, b):
        n = counters[s]
        counters[s] += 1
        ref = cent.at[s, j, pl.ds(KEEP * part, 96 - KEEP if part else KEEP)]
        cp = remote(ref, ref, cs.at[s, n], cr.at[s, part, j], plane_dev(slot(part, a, b)))
        cp.start()
        started[s].append(cp)

    def got(s, part, j):
        ref = cent.at[s, j, pl.ds(KEEP * part, 96 - KEEP if part else KEEP)]
        remote(ref, ref, cs.at[s, 0], cr.at[s, part, j], plane_dev(slot(part, 1, 0))).wait_recv()

    def launch(s, part):
        for a, b in ((1, 0), (-1, 0), (0, 1), (0, -1)):
            send(s, part, me, a, b)

    def near(s, part, sign):
        j = slot(part, -sign, 0)
        got(s, part, j)
        if (sign == 1) == (s == part):
            send(s, part, j, sign, 0)
        send(s, part, j, 0, 1)
        send(s, part, j, 0, -1)

    def far(s, part):
        j = slot(part, 2, 0)
        got(s, part, j)
        send(s, part, j, 0, 1)
        send(s, part, j, 0, -1)

    def second(s, part, d, sign):
        j = slot(part, d, -sign)
        got(s, part, j)
        if (sign == 1) == (d in (0, -1)):
            send(s, part, j, 0, sign)

    def last(s, part, d):
        got(s, part, slot(part, d, 2))

    def level(s, part, n):
        if n == 1:
            near(s, part, 1)
            near(s, part, -1)
            second(s, part, 0, 1)
            second(s, part, 0, -1)
        elif n == 2:
            far(s, part)
            for d in (1, -1):
                second(s, part, d, 1)
                second(s, part, d, -1)
            last(s, part, 0)
        elif n == 3:
            second(s, part, 2, 1)
            second(s, part, 2, -1)
            last(s, part, 1)
            last(s, part, -1)
        else:
            last(s, part, 2)

    half_copy(0).start()
    launch(0, 0)
    half_copy(1).start()

    cut = 112
    depth = samples_t.shape[0]
    low_f = pl.ds(pl.multiple_of(core * 256, 16), cut)
    high_f = pl.ds(pl.multiple_of(core * 256 + cut, 16), 256 - cut)
    sib_low = pl.ds(pl.multiple_of((1 - core) * 256, 16), cut)
    sib_high = pl.ds(pl.multiple_of((1 - core) * 256 + cut, 16), 256 - cut)
    x_samples = [
        remote(samples_t.at[low_f], peer_t.at[low_f], xs.at[2], xr.at[2], partner),
        remote(samples_t.at[high_f], peer_t.at[high_f], xs.at[3], xr.at[3], across),
    ]
    for cp in x_samples:
        cp.start()
    hand = [
        remote(peer_t.at[low_f], peer_t.at[low_f], hs.at[0], hr.at[0], sibling),
        remote(peer_t.at[high_f], peer_t.at[high_f], hs.at[1], hr.at[1], sibling),
    ]
    hand_in = [
        remote(peer_t.at[sib_low], peer_t.at[sib_low], hs.at[0], hr.at[0], sibling),
        remote(peer_t.at[sib_high], peer_t.at[sib_high], hs.at[1], hr.at[1], sibling),
    ]

    for i in (4, 5, 6):
        fetch[i].wait()
    xf = samples[...].astype(F32)
    sq = xf * xf
    sq_hi = sq.astype(BF16)
    sq_lo = (sq - sq_hi.astype(F32)).astype(BF16)
    ones = jnp.ones((16, depth), BF16)
    norm = (lax.dot_general(ones, sq_hi, NT, preferred_element_type=F32)
            + lax.dot_general(ones, sq_lo, NT, preferred_element_type=F32))
    w = weights[...]
    auxes[0] = jnp.where(iota((8, 1024), 0) == 0, w, -scale * norm[0:8])
    weighted[...] = (w * (targets[...] - preds[...])).astype(BF16)
    wt[:, 0:1024] = weighted[...]

    def weight_rows(half):
        v = auxes[half, 0:1]
        hi = v.astype(BF16).astype(F32)
        which = iota((16, 1024), 0)
        full = jnp.where(which == 0, hi, jnp.where(which == 1, v - hi, 0.0))
        wcat[:, half * 1024 : (half + 1) * 1024] = full.astype(BF16)

    weight_rows(0)
    x_rows = [
        remote(auxes.at[0], auxes.at[1], xs.at[4], xr.at[4], partner),
        remote(weighted, peer_wt, xs.at[5], xr.at[5], partner),
    ]
    for cp in x_rows:
        cp.start()

    half_copy(0).wait_recv()
    launch(0, 1)

    fetch[3].wait()
    parts = split3(coefs[...])
    for s in range(2):
        own_coef[s] = sum3(lax.dot_general(parts, select[s * 128 : (s + 1) * 128, :], NT,
                                           preferred_element_type=F32))
    x_coef = remote(own_coef, peer_coef, xs.at[6], xr.at[6], partner)
    x_coef.start()

    def l_copy(k):
        return remote(place, places.at[c], ls.at[k], lr.at[c], (r, lax.rem(c + k, 4)))

    def share_place(k, carry):
        l_copy(k).start()
        return carry

    places[c] = place[...]

    def tiles(s, half, first, stop):
        src = samples_t if half == 0 else peer_t
        base = half * 1024

        def body(k, carry):
            g = lax.rem(z + k + k // 2 - 2 * (k // 3), 4)
            picked = cent[s, pl.ds(g * 4, 4)].reshape(384, 512)
            wide = picked.astype(F32)
            a = shift - scale * jnp.sum(wide * wide, axis=1, keepdims=True)
            for i in range(4):
                prod = jnp.dot(picked, src[:, i * 256 : (i + 1) * 256], preferred_element_type=F32)
                b = auxes[half, 1:2, i * 256 : (i + 1) * 256]
                val = jnp.exp2(prod * (2.0 * scale) + (a + b)).astype(BF16)
                lo = base + i * 256
                for q in range(4):
                    kt[s, g * 4 + q, 0:96, lo : lo + 256] = val[q * 96 : (q + 1) * 96]
            for q in (0, 2):
                k2 = kt[s, pl.ds(g * 4 + q, 2), :, base : base + 1024].reshape(256, 1024)
                part = lax.dot_general(wcat[:, base : base + 1024], k2 * k2, NT, preferred_element_type=F32)
                tot = jnp.broadcast_to(part[0:1] + part[1:2], (8, 256))
                for h in range(2):
                    now = tot[:, h * 128 : (h + 1) * 128]
                    if half == 0:
                        sqsend[s, g * 4 + q + h] = now
                    else:
                        sqsend[s, g * 4 + q + h] += now
            return carry

        lax.fori_loop(first, stop, body, 0)

    def s_copy(s, j):
        return remote(sqsend.at[s, j], sqrecv.at[s, me], ss.at[s, j], sr.at[s, me], plane_dev(j))

    def push_squares(s):
        def body(k, carry):
            s_copy(s, lax.rem(me + k, 16)).start()
            return carry

        lax.fori_loop(1, 16, body, 0)

    def g_copy(s, j):
        return remote(gsend.at[s, j], grecv.at[s, me], gs.at[s, j], gr.at[s, me], plane_dev(j))

    def gradient(s, lhs):
        def pair(j2):
            k = kt[s, pl.ds(j2 * 2, 2)].reshape(256, 2048)
            g = lax.dot_general(lhs, k, NT, preferred_element_type=F32).astype(BF16)
            gsend[s, j2 * 2] = g[:, 0:128]
            gsend[s, j2 * 2 + 1] = g[:, 128:256]

        def body(k, carry):
            j2 = wrap(z + offset_of(k // 2)) * 2 + lax.rem(y // 2 + 1 + k, 2)
            pair(j2)
            g_copy(s, j2 * 2).start()
            g_copy(s, j2 * 2 + 1).start()
            return carry

        lax.fori_loop(0, 7, body, 0)
        pair(me // 2)
        g_copy(s, me + 1 - 2 * lax.rem(me, 2)).start()

    def d_copy(s, j):
        return remote(dlow.at[s, me], dlow.at[s, me], ds_.at[s, j], dr.at[s, me], plane_dev(j))

    def f_copy(s, k):
        return remote(dall.at[s, e], dall.at[s, e], fs.at[s, k], fr.at[s, e], ring_dev(k))

    def make_delta(s):
        def square(k, total):
            j = lax.rem(me + k, 16)
            remote(sqsend.at[s, j], sqrecv.at[s, j], ss.at[s, j], sr.at[s, j], plane_dev(j)).wait_recv()
            return total + sqrecv[s, j]

        lane = iota((16, 128), 1)
        coef = jnp.where(lane < KEEP, own_coef[s], peer_coef[s])
        col_square = lax.fori_loop(1, 16, square, sqsend[s, me])
        inverse = 1.0 / (col_square[0:1] + RIDGE)

        def body(k, total):
            j = lax.rem(me + k, 16)
            remote(gsend.at[s, j], grecv.at[s, j], gs.at[s, j], gr.at[s, j], plane_dev(j)).wait_recv()
            return total + grecv[s, j].astype(F32)

        total = lax.fori_loop(1, 16, body, gsend[s, me].astype(F32) - RIDGE * coef)
        delta = total * inverse
        dlow[s, me] = delta.astype(BF16)
        dall[s, e] = delta

        def push(k, carry):
            d_copy(s, peer_of(k)).start()
            return carry

        lax.fori_loop(0, 15, push, 0)

    def push_delta(s):
        def push_ring(k, carry):
            f_copy(s, lax.rem(e + k, 8)).start()
            return carry

        lax.fori_loop(1, 8, push_ring, 0)

    def wait_delta(s):
        def body(k, carry):
            j = lax.rem(me + k, 16)
            remote(dlow.at[s, j], dlow.at[s, j], ds_.at[s, j], dr.at[s, j], plane_dev(j)).wait_recv()
            return carry

        lax.fori_loop(1, 16, body, 0)
        return jnp.concatenate([dlow[s, j] for j in range(16)], axis=1)

    def p_copy(to):
        return remote(psend.at[to], precv.at[e], ps.at[to], pr.at[e], ring_dev(to))

    def change(d):
        def chunk(to):
            rel = lax.rem(to // 4 + xl, 2) * 4 + lax.rem(to, 4)
            k = kt[0, :, :, pl.ds(pl.multiple_of(rel * 256, 256), 256)].reshape(2048, 256)
            psend[to] = jnp.dot(d, k, preferred_element_type=F32).astype(BF16)

        def body(k, carry):
            to = ring_of(k)
            chunk(to)
            p_copy(to).start()
            return carry

        lax.fori_loop(0, 7, body, 0)
        chunk(e)

    def sum_change():
        def body(k, total):
            j = lax.rem(e + k, 8)
            remote(psend.at[j], precv.at[j], ps.at[j], pr.at[j], ring_dev(j)).wait_recv()
            return total + precv[j].astype(F32)

        return lax.fori_loop(1, 8, body, psend[e].astype(F32))

    def update_coefs(s, base):
        def body(k, carry):
            j = lax.rem(e + k, 8)
            remote(dall.at[s, j], dall.at[s, j], fs.at[s, j], fr.at[s, j], ring_dev(j)).wait_recv()
            return carry

        lax.fori_loop(1, 8, body, 0)
        lane = iota((16, 128), 1)
        pieces, cols = [], []
        for k in range(4):
            own = dall[s, xl * 4 + k]
            other = dall[s, (1 - xl) * 4 + k]
            pieces.append(jnp.where(lane < KEEP, own, other))
            cols.append(jnp.broadcast_to(places[k, s, 0:1], (128, 128)).T)
        lhs = split3(jnp.concatenate(pieces, axis=1))
        col = jnp.concatenate(cols, axis=0)

        def step(k, carry):
            at = pl.ds(pl.multiple_of(k * 512, 512), 512)
            base_lane = (k * 512).astype(F32)
            hot = []
            for i in range(4):
                lanes = iota((512, 128), 1).astype(F32) + (base_lane + i * 128.0)
                hot.append((col == lanes).astype(F32).astype(BF16))
            three = jnp.dot(lhs, jnp.concatenate(hot, axis=1), preferred_element_type=F32)
            coef_out[:, at] = base[:, at] + sum3(three)
            return carry

        lax.fori_loop(0, 8, step, 0)

    level(0, 0, 1)
    for s in range(2):
        for j in range(16):
            kt[s, j, 96:128, :] = jnp.zeros((32, 2048), BF16)
    level(0, 0, 2)
    level(0, 1, 1)
    level(0, 0, 3)
    level(0, 1, 2)
    tiles(0, 0, 0, 1)
    launch(1, 0)
    half_copy(1).wait_recv()
    launch(1, 1)
    level(0, 0, 4)
    for i in range(2):
        x_samples[i].wait_recv()
        hand[i].start()
    level(0, 1, 3)
    tiles(0, 0, 1, 3)
    level(1, 0, 1)
    level(1, 1, 1)
    x_rows[0].wait_recv()
    x_rows[1].wait_recv()
    weight_rows(1)
    wt[:, 1024:2048] = peer_wt[...]
    for i in range(2):
        hand_in[i].wait_recv()
    lax.fori_loop(1, 4, share_place, 0)
    tiles(0, 1, 0, 3)
    level(0, 1, 4)
    tiles(0, 0, 3, 4)
    tiles(0, 1, 3, 4)
    push_squares(0)
    gradient(0, wt[...])
    level(1, 0, 2)
    level(1, 1, 2)
    tiles(1, 0, 0, 1)
    tiles(1, 1, 0, 1)
    x_coef.wait_recv()
    make_delta(0)
    level(1, 0, 3)
    level(1, 1, 3)
    push_delta(0)
    tiles(1, 0, 1, 3)
    tiles(1, 1, 1, 2)
    change(wait_delta(0))
    level(1, 0, 4)
    level(1, 1, 4)
    tiles(1, 1, 2, 3)
    tiles(1, 0, 3, 4)
    chunk_at = pl.ds(pl.multiple_of(c * 256, 256), 256)
    pred = preds[:, chunk_at] + sum_change()

    def rel_to(to):
        return lax.rem(to // 4 + xl, 2) * 4 + c

    def w_copy(to):
        return remote(wt2.at[c], wt2.at[rel_to(to)], ws.at[to], wr.at[rel_to(to)], ring_dev(to))

    wt2[c] = (weights[:, chunk_at] * (targets[:, chunk_at] - pred)).astype(BF16)

    def push_w(k, carry):
        w_copy(ring_of(k)).start()
        return carry

    lax.fori_loop(0, 7, push_w, 0)
    pmid[c] = pred

    def q_copy(k):
        to = lax.rem(c + k, 4)
        return remote(pmid.at[c], pmid.at[c], qs.at[to], qr.at[c], (r, to))

    def push_q(k, carry):
        q_copy(k).start()
        return carry

    tiles(1, 1, 3, 4)
    push_squares(1)

    def wait_w(k, carry):
        j = lax.rem(c + k, 8)
        remote(wt2.at[j], wt2.at[j], ws.at[j], wr.at[j], ring_dev(j)).wait_recv()
        return carry

    lax.fori_loop(1, 8, wait_w, 0)
    gradient(1, jnp.concatenate([wt2[j] for j in range(8)], axis=1))
    lax.fori_loop(1, 4, push_q, 0)

    def wait_place(k, carry):
        j = lax.rem(c + k, 4)
        remote(place, places.at[j], ls.at[k], lr.at[j], (r, j)).wait_recv()
        return carry

    lax.fori_loop(1, 4, wait_place, 0)
    update_coefs(0, coefs)
    for s in range(2):
        half_copy(s).wait_send()
        for cp in started[s]:
            cp.wait_send()
    for cp in (*x_samples, *x_rows, x_coef, *hand):
        cp.wait_send()

    def drain_plane(s):
        def body(k, carry):
            j = lax.rem(me + k, 16)
            g_copy(s, j).wait_send()
            s_copy(s, j).wait_send()
            d_copy(s, j).wait_send()
            return carry

        lax.fori_loop(1, 16, body, 0)

    def drain_ring(k, carry):
        j = lax.rem(e + k, 8)
        f_copy(0, j).wait_send()
        p_copy(j).wait_send()
        w_copy(j).wait_send()
        return carry

    def drain_cent(k, carry):
        l_copy(k).wait_send()
        return carry

    drain_plane(0)
    lax.fori_loop(1, 8, drain_ring, 0)
    lax.fori_loop(1, 4, drain_cent, 0)
    make_delta(1)
    push_delta(1)
    d = wait_delta(1)

    def e_copy(rel, half, across_x):
        to_xl = xl if rel == 0 else 1 - xl
        to_hi = c // 2 if across_x == 0 else 1 - c // 2
        n = (rel * 2 + half) * 2 + across_x
        dev = (to_xl * 16 + me, to_hi * 2 + half)
        return remote(lsend.at[rel * 2 + half], lrecv.at[e], es.at[n], er.at[e], dev)

    for rel in range(2):
        for half in range(2):
            k = kt[1, :, :, rel * 1024 + half * 512 : rel * 1024 + half * 512 + 512].reshape(2048, 512)
            lsend[rel * 2 + half] = jnp.dot(d, k, preferred_element_type=F32).astype(BF16)
            e_copy(rel, half, 1).start()
            if rel == 1:
                e_copy(rel, half, 0).start()
            else:
                pl.when(core != half)(lambda half=half: e_copy(0, half, 0).start())
    lrecv[e] = lsend[core]
    update_coefs(1, coef_out)
    store_coef = pltpu.make_async_copy(coef_out, coef_hbm, loads.at[7])
    store_coef.start()
    def drain_last(k, carry):
        f_copy(1, lax.rem(e + k, 8)).wait_send()
        return carry

    def drain_mid(k, carry):
        q_copy(k).wait_send()
        return carry

    drain_plane(1)
    lax.fori_loop(1, 8, drain_last, 0)
    lax.fori_loop(1, 4, drain_mid, 0)

    def wait_q(k, carry):
        j = lax.rem(c + k, 4)
        remote(pmid.at[j], pmid.at[j], qs.at[j], qr.at[j], (r, j)).wait_recv()
        return carry

    lax.fori_loop(1, 4, wait_q, 0)

    def wait_e(k, carry):
        j = lax.rem(e + k, 8)
        remote(lrecv.at[j], lrecv.at[j], es.at[0], er.at[j], ring_dev(j)).wait_recv()
        return carry

    lax.fori_loop(1, 8, wait_e, 0)
    total = lrecv[0].astype(F32)
    for j in range(1, 8):
        total = total + lrecv[j].astype(F32)
    pend[core] = jnp.concatenate([pmid[core * 2], pmid[core * 2 + 1]], axis=1) + total
    final = remote(pend.at[core], pend.at[core], hs.at[2], hr.at[2], sibling)
    final.start()
    remote(pend.at[1 - core], pend.at[1 - core], hs.at[2], hr.at[2], sibling).wait_recv()
    pred_out[:, 0:512] = pend[0]
    pred_out[:, 512:1024] = pend[1]

    store_pred = pltpu.make_async_copy(pred_out, pred_hbm, loads.at[8])
    store_pred.start()
    for rel in range(2):
        for half in range(2):
            e_copy(rel, half, 1).wait_send()
            if rel == 1:
                e_copy(rel, half, 0).wait_send()
            else:
                pl.when(core != half)(lambda half=half: e_copy(0, half, 0).wait_send())
    final.wait_send()
    store_coef.wait()
    store_pred.wait()


def local(samples, weights, targets, predictions, centres, coefs, block_index):
    rows, depth = samples.shape
    pool = centres.shape[0]
    t = targets.shape[0]
    sharpness = 1.3 / math.sqrt(8.0 * depth)
    offset = 2.0 * depth * sharpness - 1.5 - 0.5 * math.log(rows * lax.axis_size("rows"))
    scale = sharpness * LOG2E
    shift = offset * LOG2E
    vmem = pl.BlockSpec(memory_space=pltpu.VMEM)
    hbm = pl.BlockSpec(memory_space=pl.ANY)
    sds = jax.ShapeDtypeStruct
    dma = pltpu.SemaphoreType.DMA
    pred, coef = pl.pallas_call(
        functools.partial(main_kernel, scale, shift),
        out_shape=(sds((t, rows), F32), sds((t, pool), F32)),
        in_specs=[hbm] * 7,
        out_specs=(hbm,) * 2,
        scratch_shapes=[
            pltpu.VMEM((t, rows), F32),
            pltpu.VMEM((t, pool), F32),
            pltpu.VMEM(block_index.shape, jnp.int32),
            pltpu.VMEM(centres.shape, BF16),
            pltpu.VMEM(coefs.shape, F32),
            pltpu.VMEM(samples.shape, BF16),
            pltpu.VMEM((1, rows), F32),
            pltpu.VMEM((t, rows), F32),
            pltpu.VMEM((t, rows), F32),
            pltpu.VMEM((256, pool), BF16),
            pltpu.VMEM((2, 96 - KEEP, depth), BF16),
            pltpu.VMEM((2, t, 128), F32),
            pltpu.VMEM((2, 8, 128), F32),
            pltpu.VMEM((t, rows), BF16),
            pltpu.VMEM((depth, rows), BF16),
            pltpu.VMEM((2, 16, 96, depth), BF16),
            pltpu.VMEM((depth, rows), BF16),
            pltpu.VMEM((2, t, 128), F32),
            pltpu.VMEM((4, 2, 8, 128), F32),
            pltpu.VMEM((t, 2 * rows), BF16),
            pltpu.VMEM((t, rows), BF16),
            pltpu.VMEM((2, 8, rows), F32),
            pltpu.VMEM((16, 2 * rows), BF16),
            pltpu.VMEM((2, 16, 128, 2 * rows), BF16),
            pltpu.VMEM((2, 16, t, 128), BF16),
            pltpu.VMEM((2, 16, t, 128), BF16),
            pltpu.VMEM((2, 16, 8, 128), F32),
            pltpu.VMEM((2, 16, 8, 128), F32),
            pltpu.VMEM((2, 16, t, 128), BF16),
            pltpu.VMEM((2, 8, t, 128), F32),
            pltpu.VMEM((8, t, 256), BF16),
            pltpu.VMEM((8, t, 256), BF16),
            pltpu.VMEM((4, t, 512), BF16),
            pltpu.VMEM((8, t, 512), BF16),
            pltpu.VMEM((8, t, 256), BF16),
            pltpu.VMEM((4, t, 256), F32),
            pltpu.VMEM((2, t, 512), F32),
            dma((9,)),
            dma((7,)), dma((7,)),
            dma((2, 30)), dma((2, 2, 16)),
            dma((2, 16)), dma((2, 16)),
            dma((2, 16)), dma((2, 16)),
            dma((2, 16)), dma((2, 16)),
            dma((2, 8)), dma((2, 8)),
            dma((8,)), dma((8,)),
            dma((8,)), dma((8,)),
            dma((8,)), dma((8,)),
            dma((4,)), dma((4,)),
            dma((4,)), dma((4,)),
            dma((3,)), dma((3,)),
        ],
        compiler_params=pltpu.CompilerParams(
            collective_id=0, has_side_effects=True, vmem_limit_bytes=60 * 2**20
        ),
    )(block_index, centres, coefs, samples, weights[None, :], targets, predictions)
    return coef, pred


def solution(mesh):
    in_specs = (
        P("rows", None),
        P("rows"),
        P(None, "rows"),
        P(None, "rows"),
        P("rows", None),
        P(None, "rows"),
        P(None, "cent"),
    )
    out_specs = (P(None, "rows"), P(None, "rows"))
    return jax.shard_map(local, mesh=mesh, in_specs=in_specs, out_specs=out_specs, check_vma=False)
```

```python
import functools
import math

import jax
import jax.numpy as jnp
from jax import lax
from jax.experimental import pallas as pl
from jax.experimental.pallas import tpu as pltpu
from jax.sharding import PartitionSpec as P

RIDGE = 1.0
KEEP = 64
MESH = pl.DeviceIdType.MESH
F32, BF16 = jnp.float32, jnp.bfloat16
LOG2E = 1.4426950408889634
NT = (((1,), (1,)), ((), ()))


def iota(shape, axis):
    return lax.broadcasted_iota(jnp.int32, shape, axis)


def split3(v):
    hi = v.astype(BF16)
    rest = v - hi.astype(F32)
    mid = rest.astype(BF16)
    low = (rest - mid.astype(F32)).astype(BF16)
    return jnp.concatenate([hi, mid, low], axis=0)


def sum3(v):
    return v[0:16] + v[16:32] + v[32:48]


def main_kernel(scale, shift, blk_in, centres_in, coefs_in, samples_in, weights_in, targets_in, preds_in,
                out_hbm, pred_out, coef_out,
                blk, centres, coefs, samples, weights, targets, preds, select,
                outgoing, own_coef, place, weighted, samples_t,
                cent, peer_t, peer_coef, places, wt, peer_wt, auxes, wcat, kt, gsend, grecv, sqsend, sqrecv,
                dlow, dall, psend, precv, lsend, lrecv, wt2, pmid, pend,
                loads, xs, xr, cs, cr, gs, gr, ss, sr, ds_, dr, fs, fr, ps, pr, es, er, ws, wr, qs, qr, ls, lr,
                hs, hr):
    r = lax.axis_index("rows")
    c = lax.axis_index("cent")
    xl = r // 16
    me = lax.rem(r, 16)
    z = me // 4
    y = lax.rem(me, 4)
    e = xl * 4 + c
    core = lax.rem(c, 2)

    def wrap(v):
        return lax.rem(v + 8, 4)

    def offset_of(i):
        return 2 - i + 3 * (i // 2) - 2 * (i // 3)

    def peer_of(k):
        return wrap(z + offset_of(k // 4)) * 4 + wrap(y + offset_of(lax.rem(k, 4)))

    def ring_of(k):
        m = k + 2 - 7 * (k // 6) - 2 * (k // 7)
        hi = lax.rem(c // 2 + m // 2, 2)
        return lax.rem(xl + m // 4, 2) * 4 + hi * 2 + lax.rem(c + m, 2)

    def plane_dev(j):
        return (xl * 16 + j, c)

    def ring_dev(k):
        return ((k // 4) * 16 + me, lax.rem(k, 4))

    pairs = ((blk_in, blk), (centres_in, centres), (samples_in, samples), (coefs_in, coefs),
             (weights_in, weights), (targets_in, targets), (preds_in, preds))
    fetch = [pltpu.make_async_copy(src, dst, loads.at[i]) for i, (src, dst) in enumerate(pairs)]
    for cp in fetch:
        cp.start()

    barrier = pltpu.get_barrier_semaphore()

    neighbours = (
        plane_dev(z * 4 + wrap(y + 1)),
        plane_dev(z * 4 + wrap(y - 1)),
        plane_dev(wrap(z + 1) * 4 + y),
        plane_dev(wrap(z - 1) * 4 + y),
        ((1 - xl) * 16 + me, c),
        ((1 - xl) * 16 + me, lax.rem(c + 2, 4)),
        (r, c + 1 - 2 * core),
    )
    for dev in neighbours:
        pl.semaphore_signal(barrier, inc=1, device_id=dev, device_id_type=MESH)

    pool = centres.shape[0]
    q_rows = blk.shape[1] // 128
    upper = (iota((128, 128), 0) <= iota((128, 128), 1)).astype(F32)
    lower = (iota((q_rows, q_rows), 0) > iota((q_rows, q_rows), 1)).astype(F32)
    rank_of = iota((128, 128), 0).astype(F32)
    fetch[0].wait()
    for s in range(2):
        index = jnp.concatenate([blk[s : s + 1, q * 128 : (q + 1) * 128] for q in range(q_rows)], axis=0)
        at = index - r * pool
        mine = jnp.logical_and(at >= 0, at < pool)
        flag = mine.astype(F32)
        inner = jnp.dot(flag, upper, preferred_element_type=F32)
        before = jnp.sum(jnp.dot(lower, flag, preferred_element_type=F32), axis=1, keepdims=True)
        rank = jnp.where(mine, inner + before - 1.0, -1.0)
        at_f = at.astype(F32)
        acc = jnp.zeros((128, 128), F32)
        for q in range(q_rows):
            acc = acc + jnp.where(rank[q : q + 1, :] == rank_of, at_f[q : q + 1, :], 0.0)
        col = jnp.where(iota((128, 1), 0) < 96, jnp.sum(acc, axis=1, keepdims=True), -1.0)
        row = jnp.where(iota((1, 128), 1) < 96, jnp.sum(acc.T, axis=0, keepdims=True), -1.0)
        place[s] = jnp.broadcast_to(row, (8, 128))
        for k in range(0, pool, 512):
            lanes = (iota((128, 512), 1) + k).astype(F32)
            select[s * 128 : (s + 1) * 128, k : k + 512] = (col == lanes).astype(F32).astype(BF16)
    fetch[1].wait()
    rows = jnp.dot(select[...], centres[...], preferred_element_type=F32).astype(BF16)
    for s in range(2):
        cent[s, me, 0:KEEP] = rows[s * 128 : s * 128 + KEEP]
        outgoing[s] = rows[s * 128 + KEEP : s * 128 + 96]
    fetch[2].wait()
    samples_t[...] = samples[...].T

    pl.semaphore_wait(barrier, len(neighbours))

    def remote(src, dst, ssem, rsem, dev):
        return pltpu.make_async_remote_copy(src_ref=src, dst_ref=dst, send_sem=ssem, recv_sem=rsem,
                                            device_id=dev, device_id_type=MESH)

    partner = ((1 - xl) * 16 + me, c)
    across = ((1 - xl) * 16 + me, lax.rem(c + 2, 4))
    sibling = (r, c + 1 - 2 * core)

    def half_copy(s):
        return remote(outgoing.at[s], cent.at[s, me, pl.ds(KEEP, 96 - KEEP)], xs.at[s], xr.at[s], partner)

    counters = [0, 0]
    started = [[], []]

    def slot(part, a, b):
        if part == 0:
            return wrap(z + b) * 4 + wrap(y + a)
        return wrap(z + a) * 4 + wrap(y + b)

    def send(s, part, j, a, b):
        n = counters[s]
        counters[s] += 1
        ref = cent.at[s, j, pl.ds(KEEP * part, 96 - KEEP if part else KEEP)]
        cp = remote(ref, ref, cs.at[s, n], cr.at[s, part, j], plane_dev(slot(part, a, b)))
        cp.start()
        started[s].append(cp)

    def got(s, part, j):
        ref = cent.at[s, j, pl.ds(KEEP * part, 96 - KEEP if part else KEEP)]
        remote(ref, ref, cs.at[s, 0], cr.at[s, part, j], plane_dev(slot(part, 1, 0))).wait_recv()

    def launch(s, part):
        for a, b in ((1, 0), (-1, 0), (0, 1), (0, -1)):
            send(s, part, me, a, b)

    def near(s, part, sign):
        j = slot(part, -sign, 0)
        got(s, part, j)
        if (sign == 1) == (s == part):
            send(s, part, j, sign, 0)
        send(s, part, j, 0, 1)
        send(s, part, j, 0, -1)

    def far(s, part):
        j = slot(part, 2, 0)
        got(s, part, j)
        send(s, part, j, 0, 1)
        send(s, part, j, 0, -1)

    def second(s, part, d, sign):
        j = slot(part, d, -sign)
        got(s, part, j)
        if (sign == 1) == (d in (0, -1)):
            send(s, part, j, 0, sign)

    def last(s, part, d):
        got(s, part, slot(part, d, 2))

    def level(s, part, n):
        if n == 1:
            near(s, part, 1)
            near(s, part, -1)
            second(s, part, 0, 1)
            second(s, part, 0, -1)
        elif n == 2:
            far(s, part)
            for d in (1, -1):
                second(s, part, d, 1)
                second(s, part, d, -1)
            last(s, part, 0)
        elif n == 3:
            second(s, part, 2, 1)
            second(s, part, 2, -1)
            last(s, part, 1)
            last(s, part, -1)
        else:
            last(s, part, 2)

    half_copy(0).start()
    launch(0, 0)
    half_copy(1).start()

    cut = 112
    depth = samples_t.shape[0]
    low_f = pl.ds(pl.multiple_of(core * 256, 16), cut)
    high_f = pl.ds(pl.multiple_of(core * 256 + cut, 16), 256 - cut)
    sib_low = pl.ds(pl.multiple_of((1 - core) * 256, 16), cut)
    sib_high = pl.ds(pl.multiple_of((1 - core) * 256 + cut, 16), 256 - cut)
    x_samples = [
        remote(samples_t.at[low_f], peer_t.at[low_f], xs.at[2], xr.at[2], partner),
        remote(samples_t.at[high_f], peer_t.at[high_f], xs.at[3], xr.at[3], across),
    ]
    for cp in x_samples:
        cp.start()
    hand = [
        remote(peer_t.at[low_f], peer_t.at[low_f], hs.at[0], hr.at[0], sibling),
        remote(peer_t.at[high_f], peer_t.at[high_f], hs.at[1], hr.at[1], sibling),
    ]
    hand_in = [
        remote(peer_t.at[sib_low], peer_t.at[sib_low], hs.at[0], hr.at[0], sibling),
        remote(peer_t.at[sib_high], peer_t.at[sib_high], hs.at[1], hr.at[1], sibling),
    ]

    for i in (4, 5, 6):
        fetch[i].wait()
    xf = samples[...].astype(F32)
    sq = xf * xf
    sq_hi = sq.astype(BF16)
    sq_lo = (sq - sq_hi.astype(F32)).astype(BF16)
    ones = jnp.ones((16, depth), BF16)
    norm = (lax.dot_general(ones, sq_hi, NT, preferred_element_type=F32)
            + lax.dot_general(ones, sq_lo, NT, preferred_element_type=F32))
    w = weights[...]
    auxes[0] = jnp.where(iota((8, 1024), 0) == 0, w, -scale * norm[0:8])
    weighted[...] = (w * (targets[...] - preds[...])).astype(BF16)
    wt[:, 0:1024] = weighted[...]

    def weight_rows(half):
        v = auxes[half, 0:1]
        hi = v.astype(BF16).astype(F32)
        which = iota((16, 1024), 0)
        full = jnp.where(which == 0, hi, jnp.where(which == 1, v - hi, 0.0))
        wcat[:, half * 1024 : (half + 1) * 1024] = full.astype(BF16)

    weight_rows(0)
    x_rows = [
        remote(auxes.at[0], auxes.at[1], xs.at[4], xr.at[4], partner),
        remote(weighted, peer_wt, xs.at[5], xr.at[5], partner),
    ]
    for cp in x_rows:
        cp.start()

    half_copy(0).wait_recv()
    launch(0, 1)

    fetch[3].wait()
    parts = split3(coefs[...])
    for s in range(2):
        own_coef[s] = sum3(lax.dot_general(parts, select[s * 128 : (s + 1) * 128, :], NT,
                                           preferred_element_type=F32))
    x_coef = remote(own_coef, peer_coef, xs.at[6], xr.at[6], partner)
    x_coef.start()

    def l_copy(k):
        return remote(place, places.at[c], ls.at[k], lr.at[c], (r, lax.rem(c + k, 4)))

    def share_place(k, carry):
        l_copy(k).start()
        return carry

    places[c] = place[...]

    def tiles(s, half, first, stop):
        src = samples_t if half == 0 else peer_t
        base = half * 1024

        def body(k, carry):
            g = lax.rem(z + k + k // 2 - 2 * (k // 3), 4)
            picked = cent[s, pl.ds(g * 4, 4)].reshape(384, 512)
            wide = picked.astype(F32)
            a = shift - scale * jnp.sum(wide * wide, axis=1, keepdims=True)
            for i in range(4):
                prod = jnp.dot(picked, src[:, i * 256 : (i + 1) * 256], preferred_element_type=F32)
                b = auxes[half, 1:2, i * 256 : (i + 1) * 256]
                val = jnp.exp2(prod * (2.0 * scale) + (a + b)).astype(BF16)
                lo = base + i * 256
                for q in range(4):
                    kt[s, g * 4 + q, 0:96, lo : lo + 256] = val[q * 96 : (q + 1) * 96]
            for q in (0, 2):
                k2 = kt[s, pl.ds(g * 4 + q, 2), :, base : base + 1024].reshape(256, 1024)
                part = lax.dot_general(wcat[:, base : base + 1024], k2 * k2, NT, preferred_element_type=F32)
                tot = jnp.broadcast_to(part[0:1] + part[1:2], (8, 256))
                for h in range(2):
                    now = tot[:, h * 128 : (h + 1) * 128]
                    if half == 0:
                        sqsend[s, g * 4 + q + h] = now
                    else:
                        sqsend[s, g * 4 + q + h] += now
            return carry

        lax.fori_loop(first, stop, body, 0)

    def s_copy(s, j):
        return remote(sqsend.at[s, j], sqrecv.at[s, me], ss.at[s, j], sr.at[s, me], plane_dev(j))

    def push_squares(s):
        def body(k, carry):
            s_copy(s, lax.rem(me + k, 16)).start()
            return carry

        lax.fori_loop(1, 16, body, 0)

    def g_copy(s, j):
        return remote(gsend.at[s, j], grecv.at[s, me], gs.at[s, j], gr.at[s, me], plane_dev(j))

    def gradient(s, lhs):
        def pair(j2):
            k = kt[s, pl.ds(j2 * 2, 2)].reshape(256, 2048)
            g = lax.dot_general(lhs, k, NT, preferred_element_type=F32).astype(BF16)
            gsend[s, j2 * 2] = g[:, 0:128]
            gsend[s, j2 * 2 + 1] = g[:, 128:256]

        def body(k, carry):
            j2 = wrap(z + offset_of(k // 2)) * 2 + lax.rem(y // 2 + 1 + k, 2)
            pair(j2)
            g_copy(s, j2 * 2).start()
            g_copy(s, j2 * 2 + 1).start()
            return carry

        lax.fori_loop(0, 7, body, 0)
        pair(me // 2)
        g_copy(s, me + 1 - 2 * lax.rem(me, 2)).start()

    def d_copy(s, j):
        return remote(dlow.at[s, me], dlow.at[s, me], ds_.at[s, j], dr.at[s, me], plane_dev(j))

    def f_copy(s, k):
        return remote(dall.at[s, e], dall.at[s, e], fs.at[s, k], fr.at[s, e], ring_dev(k))

    def make_delta(s):
        def square(k, total):
            j = lax.rem(me + k, 16)
            remote(sqsend.at[s, j], sqrecv.at[s, j], ss.at[s, j], sr.at[s, j], plane_dev(j)).wait_recv()
            return total + sqrecv[s, j]

        lane = iota((16, 128), 1)
        coef = jnp.where(lane < KEEP, own_coef[s], peer_coef[s])
        col_square = lax.fori_loop(1, 16, square, sqsend[s, me])
        inverse = 1.0 / (col_square[0:1] + RIDGE)

        def body(k, total):
            j = lax.rem(me + k, 16)
            remote(gsend.at[s, j], grecv.at[s, j], gs.at[s, j], gr.at[s, j], plane_dev(j)).wait_recv()
            return total + grecv[s, j].astype(F32)

        total = lax.fori_loop(1, 16, body, gsend[s, me].astype(F32) - RIDGE * coef)
        delta = total * inverse
        dlow[s, me] = delta.astype(BF16)
        dall[s, e] = delta

        def push(k, carry):
            d_copy(s, peer_of(k)).start()
            return carry

        lax.fori_loop(0, 15, push, 0)

    def push_delta(s):
        def push_ring(k, carry):
            f_copy(s, lax.rem(e + k, 8)).start()
            return carry

        lax.fori_loop(1, 8, push_ring, 0)

    def wait_delta(s):
        def body(k, carry):
            j = lax.rem(me + k, 16)
            remote(dlow.at[s, j], dlow.at[s, j], ds_.at[s, j], dr.at[s, j], plane_dev(j)).wait_recv()
            return carry

        lax.fori_loop(1, 16, body, 0)
        return jnp.concatenate([dlow[s, j] for j in range(16)], axis=1)

    def p_copy(to):
        return remote(psend.at[to], precv.at[e], ps.at[to], pr.at[e], ring_dev(to))

    def change(d):
        def chunk(to):
            rel = lax.rem(to // 4 + xl, 2) * 4 + lax.rem(to, 4)
            k = kt[0, :, :, pl.ds(pl.multiple_of(rel * 256, 256), 256)].reshape(2048, 256)
            psend[to] = jnp.dot(d, k, preferred_element_type=F32).astype(BF16)

        def body(k, carry):
            to = ring_of(k)
            chunk(to)
            p_copy(to).start()
            return carry

        lax.fori_loop(0, 7, body, 0)
        chunk(e)

    def sum_change():
        def body(k, total):
            j = lax.rem(e + k, 8)
            remote(psend.at[j], precv.at[j], ps.at[j], pr.at[j], ring_dev(j)).wait_recv()
            return total + precv[j].astype(F32)

        return lax.fori_loop(1, 8, body, psend[e].astype(F32))

    def update_coefs(s, base):
        def body(k, carry):
            j = lax.rem(e + k, 8)
            remote(dall.at[s, j], dall.at[s, j], fs.at[s, j], fr.at[s, j], ring_dev(j)).wait_recv()
            return carry

        lax.fori_loop(1, 8, body, 0)
        lane = iota((16, 128), 1)
        pieces, cols = [], []
        for k in range(4):
            own = dall[s, xl * 4 + k]
            other = dall[s, (1 - xl) * 4 + k]
            pieces.append(jnp.where(lane < KEEP, own, other))
            cols.append(jnp.broadcast_to(places[k, s, 0:1], (128, 128)).T)
        lhs = split3(jnp.concatenate(pieces, axis=1))
        col = jnp.concatenate(cols, axis=0)

        def step(k, carry):
            at = pl.ds(pl.multiple_of(k * 512, 512), 512)
            base_lane = (k * 512).astype(F32)
            hot = []
            for i in range(4):
                lanes = iota((512, 128), 1).astype(F32) + (base_lane + i * 128.0)
                hot.append((col == lanes).astype(F32).astype(BF16))
            three = jnp.dot(lhs, jnp.concatenate(hot, axis=1), preferred_element_type=F32)
            coef_out[:, at] = base[:, at] + sum3(three)
            return carry

        lax.fori_loop(0, 8, step, 0)

    level(0, 0, 1)
    for s in range(2):
        for j in range(16):
            kt[s, j, 96:128, :] = jnp.zeros((32, 2048), BF16)
    level(0, 0, 2)
    level(0, 1, 1)
    level(0, 0, 3)
    level(0, 1, 2)
    tiles(0, 0, 0, 1)
    launch(1, 0)
    half_copy(1).wait_recv()
    launch(1, 1)
    level(0, 0, 4)
    for i in range(2):
        x_samples[i].wait_recv()
        hand[i].start()
    level(0, 1, 3)
    tiles(0, 0, 1, 3)
    level(1, 0, 1)
    level(1, 1, 1)
    x_rows[0].wait_recv()
    x_rows[1].wait_recv()
    weight_rows(1)
    wt[:, 1024:2048] = peer_wt[...]
    for i in range(2):
        hand_in[i].wait_recv()
    lax.fori_loop(1, 4, share_place, 0)
    tiles(0, 1, 0, 3)
    level(0, 1, 4)
    tiles(0, 0, 3, 4)
    tiles(0, 1, 3, 4)
    push_squares(0)
    gradient(0, wt[...])
    level(1, 0, 2)
    level(1, 1, 2)
    tiles(1, 0, 0, 1)
    tiles(1, 1, 0, 1)
    x_coef.wait_recv()
    make_delta(0)
    level(1, 0, 3)
    level(1, 1, 3)
    push_delta(0)
    tiles(1, 0, 1, 3)
    tiles(1, 1, 1, 2)
    change(wait_delta(0))
    level(1, 0, 4)
    level(1, 1, 4)
    tiles(1, 1, 2, 3)
    tiles(1, 0, 3, 4)
    chunk_at = pl.ds(pl.multiple_of(c * 256, 256), 256)
    pred = preds[:, chunk_at] + sum_change()

    def rel_to(to):
        return lax.rem(to // 4 + xl, 2) * 4 + c

    def w_copy(to):
        return remote(wt2.at[c], wt2.at[rel_to(to)], ws.at[to], wr.at[rel_to(to)], ring_dev(to))

    wt2[c] = (weights[:, chunk_at] * (targets[:, chunk_at] - pred)).astype(BF16)

    def push_w(k, carry):
        w_copy(ring_of(k)).start()
        return carry

    lax.fori_loop(0, 7, push_w, 0)
    pmid[c] = pred

    def q_copy(k):
        to = lax.rem(c + k, 4)
        return remote(pmid.at[c], pmid.at[c], qs.at[to], qr.at[c], (r, to))

    def push_q(k, carry):
        q_copy(k).start()
        return carry

    tiles(1, 1, 3, 4)
    push_squares(1)

    def wait_w(k, carry):
        j = lax.rem(c + k, 8)
        remote(wt2.at[j], wt2.at[j], ws.at[j], wr.at[j], ring_dev(j)).wait_recv()
        return carry

    lax.fori_loop(1, 8, wait_w, 0)
    gradient(1, jnp.concatenate([wt2[j] for j in range(8)], axis=1))
    lax.fori_loop(1, 4, push_q, 0)

    def wait_place(k, carry):
        j = lax.rem(c + k, 4)
        remote(place, places.at[j], ls.at[k], lr.at[j], (r, j)).wait_recv()
        return carry

    lax.fori_loop(1, 4, wait_place, 0)
    update_coefs(0, coefs)
    for s in range(2):
        half_copy(s).wait_send()
        for cp in started[s]:
            cp.wait_send()
    for cp in (*x_samples, *x_rows, x_coef, *hand):
        cp.wait_send()

    def drain_plane(s):
        def body(k, carry):
            j = lax.rem(me + k, 16)
            g_copy(s, j).wait_send()
            s_copy(s, j).wait_send()
            d_copy(s, j).wait_send()
            return carry

        lax.fori_loop(1, 16, body, 0)

    def drain_ring(k, carry):
        j = lax.rem(e + k, 8)
        f_copy(0, j).wait_send()
        p_copy(j).wait_send()
        w_copy(j).wait_send()
        return carry

    def drain_cent(k, carry):
        l_copy(k).wait_send()
        return carry

    drain_plane(0)
    lax.fori_loop(1, 8, drain_ring, 0)
    lax.fori_loop(1, 4, drain_cent, 0)
    make_delta(1)
    push_delta(1)
    d = wait_delta(1)

    def e_copy(rel, half, across_x):
        to_xl = xl if rel == 0 else 1 - xl
        to_hi = c // 2 if across_x == 0 else 1 - c // 2
        n = (rel * 2 + half) * 2 + across_x
        dev = (to_xl * 16 + me, to_hi * 2 + half)
        return remote(lsend.at[rel * 2 + half], lrecv.at[e], es.at[n], er.at[e], dev)

    for rel in range(2):
        for half in range(2):
            k = kt[1, :, :, rel * 1024 + half * 512 : rel * 1024 + half * 512 + 512].reshape(2048, 512)
            lsend[rel * 2 + half] = jnp.dot(d, k, preferred_element_type=F32).astype(BF16)
            e_copy(rel, half, 1).start()
            if rel == 1:
                e_copy(rel, half, 0).start()
            else:
                pl.when(core != half)(lambda half=half: e_copy(0, half, 0).start())
    lrecv[e] = lsend[core]
    update_coefs(1, coef_out)
    store_coef = pltpu.make_async_copy(coef_out, out_hbm.at[:, pl.ds(0, pool)], loads.at[7])
    store_coef.start()
    def drain_last(k, carry):
        f_copy(1, lax.rem(e + k, 8)).wait_send()
        return carry

    def drain_mid(k, carry):
        q_copy(k).wait_send()
        return carry

    drain_plane(1)
    lax.fori_loop(1, 8, drain_last, 0)
    lax.fori_loop(1, 4, drain_mid, 0)

    def wait_q(k, carry):
        j = lax.rem(c + k, 4)
        remote(pmid.at[j], pmid.at[j], qs.at[j], qr.at[j], (r, j)).wait_recv()
        return carry

    lax.fori_loop(1, 4, wait_q, 0)

    def wait_e(k, carry):
        j = lax.rem(e + k, 8)
        remote(lrecv.at[j], lrecv.at[j], es.at[0], er.at[j], ring_dev(j)).wait_recv()
        return carry

    lax.fori_loop(1, 8, wait_e, 0)
    total = lrecv[0].astype(F32)
    for j in range(1, 8):
        total = total + lrecv[j].astype(F32)
    pend[core] = jnp.concatenate([pmid[core * 2], pmid[core * 2 + 1]], axis=1) + total
    final = remote(pend.at[core], pend.at[core], hs.at[2], hr.at[2], sibling)
    final.start()
    remote(pend.at[1 - core], pend.at[1 - core], hs.at[2], hr.at[2], sibling).wait_recv()
    pred_out[:, 0:512] = pend[0]
    pred_out[:, 512:1024] = pend[1]

    store_pred = pltpu.make_async_copy(pred_out, out_hbm.at[:, pl.ds(pool, pred_out.shape[1])], loads.at[8])
    store_pred.start()
    for rel in range(2):
        for half in range(2):
            e_copy(rel, half, 1).wait_send()
            if rel == 1:
                e_copy(rel, half, 0).wait_send()
            else:
                pl.when(core != half)(lambda half=half: e_copy(0, half, 0).wait_send())
    final.wait_send()
    store_coef.wait()
    store_pred.wait()


def local(samples, weights, targets, predictions, centres, coefs, block_index):
    rows, depth = samples.shape
    pool = centres.shape[0]
    t = targets.shape[0]
    sharpness = 1.3 / math.sqrt(8.0 * depth)
    offset = 2.0 * depth * sharpness - 1.5 - 0.5 * math.log(rows * lax.axis_size("rows"))
    scale = sharpness * LOG2E
    shift = offset * LOG2E
    vmem = pl.BlockSpec(memory_space=pltpu.VMEM)
    hbm = pl.BlockSpec(memory_space=pl.ANY)
    sds = jax.ShapeDtypeStruct
    dma = pltpu.SemaphoreType.DMA
    both = pl.pallas_call(
        functools.partial(main_kernel, scale, shift),
        out_shape=sds((t, pool + rows), F32),
        in_specs=[hbm] * 7,
        out_specs=hbm,
        scratch_shapes=[
            pltpu.VMEM((t, rows), F32),
            pltpu.VMEM((t, pool), F32),
            pltpu.VMEM(block_index.shape, jnp.int32),
            pltpu.VMEM(centres.shape, BF16),
            pltpu.VMEM(coefs.shape, F32),
            pltpu.VMEM(samples.shape, BF16),
            pltpu.VMEM((1, rows), F32),
            pltpu.VMEM((t, rows), F32),
            pltpu.VMEM((t, rows), F32),
            pltpu.VMEM((256, pool), BF16),
            pltpu.VMEM((2, 96 - KEEP, depth), BF16),
            pltpu.VMEM((2, t, 128), F32),
            pltpu.VMEM((2, 8, 128), F32),
            pltpu.VMEM((t, rows), BF16),
            pltpu.VMEM((depth, rows), BF16),
            pltpu.VMEM((2, 16, 96, depth), BF16),
            pltpu.VMEM((depth, rows), BF16),
            pltpu.VMEM((2, t, 128), F32),
            pltpu.VMEM((4, 2, 8, 128), F32),
            pltpu.VMEM((t, 2 * rows), BF16),
            pltpu.VMEM((t, rows), BF16),
            pltpu.VMEM((2, 8, rows), F32),
            pltpu.VMEM((16, 2 * rows), BF16),
            pltpu.VMEM((2, 16, 128, 2 * rows), BF16),
            pltpu.VMEM((2, 16, t, 128), BF16),
            pltpu.VMEM((2, 16, t, 128), BF16),
            pltpu.VMEM((2, 16, 8, 128), F32),
            pltpu.VMEM((2, 16, 8, 128), F32),
            pltpu.VMEM((2, 16, t, 128), BF16),
            pltpu.VMEM((2, 8, t, 128), F32),
            pltpu.VMEM((8, t, 256), BF16),
            pltpu.VMEM((8, t, 256), BF16),
            pltpu.VMEM((4, t, 512), BF16),
            pltpu.VMEM((8, t, 512), BF16),
            pltpu.VMEM((8, t, 256), BF16),
            pltpu.VMEM((4, t, 256), F32),
            pltpu.VMEM((2, t, 512), F32),
            dma((9,)),
            dma((7,)), dma((7,)),
            dma((2, 30)), dma((2, 2, 16)),
            dma((2, 16)), dma((2, 16)),
            dma((2, 16)), dma((2, 16)),
            dma((2, 16)), dma((2, 16)),
            dma((2, 8)), dma((2, 8)),
            dma((8,)), dma((8,)),
            dma((8,)), dma((8,)),
            dma((8,)), dma((8,)),
            dma((4,)), dma((4,)),
            dma((4,)), dma((4,)),
            dma((3,)), dma((3,)),
        ],
        compiler_params=pltpu.CompilerParams(
            collective_id=0, has_side_effects=True, vmem_limit_bytes=60 * 2**20
        ),
    )(block_index, centres, coefs, samples, weights[None, :], targets, predictions)
    return both[:, :pool], both[:, pool:]


def solution(mesh):
    in_specs = (
        P("rows", None),
        P("rows"),
        P(None, "rows"),
        P(None, "rows"),
        P("rows", None),
        P(None, "rows"),
        P(None, "cent"),
    )
    out_specs = (P(None, "rows"), P(None, "rows"))
    return jax.shard_map(local, mesh=mesh, in_specs=in_specs, out_specs=out_specs, check_vma=False)
```

```python
import functools
import math

import jax
import jax.numpy as jnp
from jax import lax
from jax.experimental import pallas as pl
from jax.experimental.pallas import tpu as pltpu
from jax.sharding import PartitionSpec as P

RIDGE = 1.0
KEEP = 64
MESH = pl.DeviceIdType.MESH
F32, BF16 = jnp.float32, jnp.bfloat16
LOG2E = 1.4426950408889634
NT = (((1,), (1,)), ((), ()))


def iota(shape, axis):
    return lax.broadcasted_iota(jnp.int32, shape, axis)


def split3(v):
    hi = v.astype(BF16)
    rest = v - hi.astype(F32)
    mid = rest.astype(BF16)
    low = (rest - mid.astype(F32)).astype(BF16)
    return jnp.concatenate([hi, mid, low], axis=0)


def sum3(v):
    return v[0:16] + v[16:32] + v[32:48]


def main_kernel(scale, shift, blk_in, centres_in, coefs_in, samples_in, weights_in, targets_in, preds_in,
                pred_hbm, coef_hbm, pred_out, coef_out,
                blk, centres, coefs, samples, weights, targets, preds, select,
                outgoing, own_coef, place, weighted, samples_t,
                cent, peer_t, peer_coef, places, wt, peer_wt, auxes, wcat, kt, gsend, grecv, sqsend, sqrecv,
                dlow, dall, psend, precv, lsend, lrecv, wt2, pmid, pend,
                loads, xs, xr, cs, cr, gs, gr, ss, sr, ds_, dr, fs, fr, ps, pr, es, er, ws, wr, qs, qr, ls, lr,
                hs, hr):
    r = lax.axis_index("rows")
    c = lax.axis_index("cent")
    xl = r // 16
    me = lax.rem(r, 16)
    z = me // 4
    y = lax.rem(me, 4)
    e = xl * 4 + c
    core = lax.rem(c, 2)

    def wrap(v):
        return lax.rem(v + 8, 4)

    def offset_of(i):
        return 2 - i + 3 * (i // 2) - 2 * (i // 3)

    def peer_of(k):
        return wrap(z + offset_of(k // 4)) * 4 + wrap(y + offset_of(lax.rem(k, 4)))

    def ring_of(k):
        m = k + 2 - 7 * (k // 6) - 2 * (k // 7)
        hi = lax.rem(c // 2 + m // 2, 2)
        return lax.rem(xl + m // 4, 2) * 4 + hi * 2 + lax.rem(c + m, 2)

    def plane_dev(j):
        return (xl * 16 + j, c)

    def ring_dev(k):
        return ((k // 4) * 16 + me, lax.rem(k, 4))

    pairs = ((blk_in, blk), (centres_in, centres), (samples_in, samples), (coefs_in, coefs),
             (weights_in, weights), (targets_in, targets), (preds_in, preds))
    fetch = [pltpu.make_async_copy(src, dst, loads.at[i]) for i, (src, dst) in enumerate(pairs)]
    for cp in fetch:
        cp.start()

    barrier = pltpu.get_barrier_semaphore()

    neighbours = (
        plane_dev(z * 4 + wrap(y + 1)),
        plane_dev(z * 4 + wrap(y - 1)),
        plane_dev(wrap(z + 1) * 4 + y),
        plane_dev(wrap(z - 1) * 4 + y),
        ((1 - xl) * 16 + me, c),
        ((1 - xl) * 16 + me, lax.rem(c + 2, 4)),
        (r, c + 1 - 2 * core),
    )
    for dev in neighbours:
        pl.semaphore_signal(barrier, inc=1, device_id=dev, device_id_type=MESH)

    pool = centres.shape[0]
    q_rows = blk.shape[1] // 128
    upper = (iota((128, 128), 0) <= iota((128, 128), 1)).astype(F32)
    lower = (iota((q_rows, q_rows), 0) > iota((q_rows, q_rows), 1)).astype(F32)
    rank_of = iota((128, 128), 0).astype(F32)
    fetch[0].wait()
    def extract(s):
        index = jnp.concatenate([blk[s : s + 1, q * 128 : (q + 1) * 128] for q in range(q_rows)], axis=0)
        at = index - r * pool
        mine = jnp.logical_and(at >= 0, at < pool)
        flag = mine.astype(F32)
        inner = jnp.dot(flag, upper, preferred_element_type=F32)
        before = jnp.sum(jnp.dot(lower, flag, preferred_element_type=F32), axis=1, keepdims=True)
        rank = jnp.where(mine, inner + before - 1.0, -1.0)
        at_f = at.astype(F32)
        acc = jnp.zeros((128, 128), F32)
        for q in range(q_rows):
            acc = acc + jnp.where(rank[q : q + 1, :] == rank_of, at_f[q : q + 1, :], 0.0)
        col = jnp.where(iota((128, 1), 0) < 96, jnp.sum(acc, axis=1, keepdims=True), -1.0)
        row = jnp.where(iota((1, 128), 1) < 96, jnp.sum(acc.T, axis=0, keepdims=True), -1.0)
        place[s] = jnp.broadcast_to(row, (8, 128))
        for k in range(0, pool, 512):
            lanes = (iota((128, 512), 1) + k).astype(F32)
            select[s * 128 : (s + 1) * 128, k : k + 512] = (col == lanes).astype(F32).astype(BF16)
        rows = jnp.dot(select[s * 128 : (s + 1) * 128, :], centres[...], preferred_element_type=F32).astype(BF16)
        cent[s, me, 0:KEEP] = rows[0:KEEP]
        outgoing[s] = rows[KEEP:96]

    fetch[1].wait()
    extract(0)

    pl.semaphore_wait(barrier, len(neighbours))

    def remote(src, dst, ssem, rsem, dev):
        return pltpu.make_async_remote_copy(src_ref=src, dst_ref=dst, send_sem=ssem, recv_sem=rsem,
                                            device_id=dev, device_id_type=MESH)

    partner = ((1 - xl) * 16 + me, c)
    across = ((1 - xl) * 16 + me, lax.rem(c + 2, 4))
    sibling = (r, c + 1 - 2 * core)

    def half_copy(s):
        return remote(outgoing.at[s], cent.at[s, me, pl.ds(KEEP, 96 - KEEP)], xs.at[s], xr.at[s], partner)

    counters = [0, 0]
    started = [[], []]

    def slot(part, a, b):
        if part == 0:
            return wrap(z + b) * 4 + wrap(y + a)
        return wrap(z + a) * 4 + wrap(y + b)

    def send(s, part, j, a, b):
        n = counters[s]
        counters[s] += 1
        ref = cent.at[s, j, pl.ds(KEEP * part, 96 - KEEP if part else KEEP)]
        cp = remote(ref, ref, cs.at[s, n], cr.at[s, part, j], plane_dev(slot(part, a, b)))
        cp.start()
        started[s].append(cp)

    def got(s, part, j):
        ref = cent.at[s, j, pl.ds(KEEP * part, 96 - KEEP if part else KEEP)]
        remote(ref, ref, cs.at[s, 0], cr.at[s, part, j], plane_dev(slot(part, 1, 0))).wait_recv()

    def launch(s, part):
        for a, b in ((1, 0), (-1, 0), (0, 1), (0, -1)):
            send(s, part, me, a, b)

    def near(s, part, sign):
        j = slot(part, -sign, 0)
        got(s, part, j)
        if (sign == 1) == (s == part):
            send(s, part, j, sign, 0)
        send(s, part, j, 0, 1)
        send(s, part, j, 0, -1)

    def far(s, part):
        j = slot(part, 2, 0)
        got(s, part, j)
        send(s, part, j, 0, 1)
        send(s, part, j, 0, -1)

    def second(s, part, d, sign):
        j = slot(part, d, -sign)
        got(s, part, j)
        if (sign == 1) == (d in (0, -1)):
            send(s, part, j, 0, sign)

    def last(s, part, d):
        got(s, part, slot(part, d, 2))

    def level(s, part, n):
        if n == 1:
            near(s, part, 1)
            near(s, part, -1)
            second(s, part, 0, 1)
            second(s, part, 0, -1)
        elif n == 2:
            far(s, part)
            for d in (1, -1):
                second(s, part, d, 1)
                second(s, part, d, -1)
            last(s, part, 0)
        elif n == 3:
            second(s, part, 2, 1)
            second(s, part, 2, -1)
            last(s, part, 1)
            last(s, part, -1)
        else:
            last(s, part, 2)

    half_copy(0).start()
    launch(0, 0)
    fetch[2].wait()
    samples_t[...] = samples[...].T

    cut = 112
    depth = samples_t.shape[0]
    low_f = pl.ds(pl.multiple_of(core * 256, 16), cut)
    high_f = pl.ds(pl.multiple_of(core * 256 + cut, 16), 256 - cut)
    sib_low = pl.ds(pl.multiple_of((1 - core) * 256, 16), cut)
    sib_high = pl.ds(pl.multiple_of((1 - core) * 256 + cut, 16), 256 - cut)
    x_samples = [
        remote(samples_t.at[low_f], peer_t.at[low_f], xs.at[2], xr.at[2], partner),
        remote(samples_t.at[high_f], peer_t.at[high_f], xs.at[3], xr.at[3], across),
    ]
    for cp in x_samples:
        cp.start()
    extract(1)
    half_copy(1).start()
    hand = [
        remote(peer_t.at[low_f], peer_t.at[low_f], hs.at[0], hr.at[0], sibling),
        remote(peer_t.at[high_f], peer_t.at[high_f], hs.at[1], hr.at[1], sibling),
    ]
    hand_in = [
        remote(peer_t.at[sib_low], peer_t.at[sib_low], hs.at[0], hr.at[0], sibling),
        remote(peer_t.at[sib_high], peer_t.at[sib_high], hs.at[1], hr.at[1], sibling),
    ]

    for i in (4, 5, 6):
        fetch[i].wait()
    xf = samples[...].astype(F32)
    sq = xf * xf
    sq_hi = sq.astype(BF16)
    sq_lo = (sq - sq_hi.astype(F32)).astype(BF16)
    ones = jnp.ones((16, depth), BF16)
    norm = (lax.dot_general(ones, sq_hi, NT, preferred_element_type=F32)
            + lax.dot_general(ones, sq_lo, NT, preferred_element_type=F32))
    w = weights[...]
    auxes[0] = jnp.where(iota((8, 1024), 0) == 0, w, -scale * norm[0:8])
    weighted[...] = (w * (targets[...] - preds[...])).astype(BF16)
    wt[:, 0:1024] = weighted[...]

    def weight_rows(half):
        v = auxes[half, 0:1]
        hi = v.astype(BF16).astype(F32)
        which = iota((16, 1024), 0)
        full = jnp.where(which == 0, hi, jnp.where(which == 1, v - hi, 0.0))
        wcat[:, half * 1024 : (half + 1) * 1024] = full.astype(BF16)

    weight_rows(0)
    x_rows = [
        remote(auxes.at[0], auxes.at[1], xs.at[4], xr.at[4], partner),
        remote(weighted, peer_wt, xs.at[5], xr.at[5], partner),
    ]
    for cp in x_rows:
        cp.start()

    half_copy(0).wait_recv()
    launch(0, 1)

    fetch[3].wait()
    parts = split3(coefs[...])
    for s in range(2):
        own_coef[s] = sum3(lax.dot_general(parts, select[s * 128 : (s + 1) * 128, :], NT,
                                           preferred_element_type=F32))
    x_coef = remote(own_coef, peer_coef, xs.at[6], xr.at[6], partner)
    x_coef.start()

    def l_copy(k):
        return remote(place, places.at[c], ls.at[k], lr.at[c], (r, lax.rem(c + k, 4)))

    def share_place(k, carry):
        l_copy(k).start()
        return carry

    places[c] = place[...]

    def tiles(s, half, first, stop):
        src = samples_t if half == 0 else peer_t
        base = half * 1024

        def body(k, carry):
            g = lax.rem(z + k + k // 2 - 2 * (k // 3), 4)
            picked = cent[s, pl.ds(g * 4, 4)].reshape(384, 512)
            wide = picked.astype(F32)
            a = shift - scale * jnp.sum(wide * wide, axis=1, keepdims=True)
            for i in range(4):
                prod = jnp.dot(picked, src[:, i * 256 : (i + 1) * 256], preferred_element_type=F32)
                b = auxes[half, 1:2, i * 256 : (i + 1) * 256]
                val = jnp.exp2(prod * (2.0 * scale) + (a + b)).astype(BF16)
                lo = base + i * 256
                for q in range(4):
                    kt[s, g * 4 + q, 0:96, lo : lo + 256] = val[q * 96 : (q + 1) * 96]
            for q in (0, 2):
                k2 = kt[s, pl.ds(g * 4 + q, 2), :, base : base + 1024].reshape(256, 1024)
                part = lax.dot_general(wcat[:, base : base + 1024], k2 * k2, NT, preferred_element_type=F32)
                tot = jnp.broadcast_to(part[0:1] + part[1:2], (8, 256))
                for h in range(2):
                    now = tot[:, h * 128 : (h + 1) * 128]
                    if half == 0:
                        sqsend[s, g * 4 + q + h] = now
                    else:
                        sqsend[s, g * 4 + q + h] += now
            return carry

        lax.fori_loop(first, stop, body, 0)

    def s_copy(s, j):
        return remote(sqsend.at[s, j], sqrecv.at[s, me], ss.at[s, j], sr.at[s, me], plane_dev(j))

    def push_squares(s):
        def body(k, carry):
            s_copy(s, lax.rem(me + k, 16)).start()
            return carry

        lax.fori_loop(1, 16, body, 0)

    def g_copy(s, j):
        return remote(gsend.at[s, j], grecv.at[s, me], gs.at[s, j], gr.at[s, me], plane_dev(j))

    def gradient(s, lhs):
        def pair(j2):
            k = kt[s, pl.ds(j2 * 2, 2)].reshape(256, 2048)
            g = lax.dot_general(lhs, k, NT, preferred_element_type=F32).astype(BF16)
            gsend[s, j2 * 2] = g[:, 0:128]
            gsend[s, j2 * 2 + 1] = g[:, 128:256]

        def body(k, carry):
            j2 = wrap(z + offset_of(k // 2)) * 2 + lax.rem(y // 2 + 1 + k, 2)
            pair(j2)
            g_copy(s, j2 * 2).start()
            g_copy(s, j2 * 2 + 1).start()
            return carry

        lax.fori_loop(0, 7, body, 0)
        pair(me // 2)
        g_copy(s, me + 1 - 2 * lax.rem(me, 2)).start()

    def d_copy(s, j):
        return remote(dlow.at[s, me], dlow.at[s, me], ds_.at[s, j], dr.at[s, me], plane_dev(j))

    def f_copy(s, k):
        return remote(dall.at[s, e], dall.at[s, e], fs.at[s, k], fr.at[s, e], ring_dev(k))

    def make_delta(s):
        def square(k, total):
            j = lax.rem(me + k, 16)
            remote(sqsend.at[s, j], sqrecv.at[s, j], ss.at[s, j], sr.at[s, j], plane_dev(j)).wait_recv()
            return total + sqrecv[s, j]

        lane = iota((16, 128), 1)
        coef = jnp.where(lane < KEEP, own_coef[s], peer_coef[s])
        col_square = lax.fori_loop(1, 16, square, sqsend[s, me])
        inverse = 1.0 / (col_square[0:1] + RIDGE)

        def body(k, total):
            j = lax.rem(me + k, 16)
            remote(gsend.at[s, j], grecv.at[s, j], gs.at[s, j], gr.at[s, j], plane_dev(j)).wait_recv()
            return total + grecv[s, j].astype(F32)

        total = lax.fori_loop(1, 16, body, gsend[s, me].astype(F32) - RIDGE * coef)
        delta = total * inverse
        dlow[s, me] = delta.astype(BF16)
        dall[s, e] = delta

        def push(k, carry):
            d_copy(s, peer_of(k)).start()
            return carry

        lax.fori_loop(0, 15, push, 0)

    def push_delta(s):
        def push_ring(k, carry):
            f_copy(s, lax.rem(e + k, 8)).start()
            return carry

        lax.fori_loop(1, 8, push_ring, 0)

    def wait_delta(s):
        def body(k, carry):
            j = lax.rem(me + k, 16)
            remote(dlow.at[s, j], dlow.at[s, j], ds_.at[s, j], dr.at[s, j], plane_dev(j)).wait_recv()
            return carry

        lax.fori_loop(1, 16, body, 0)
        return jnp.concatenate([dlow[s, j] for j in range(16)], axis=1)

    def p_copy(to):
        return remote(psend.at[to], precv.at[e], ps.at[to], pr.at[e], ring_dev(to))

    def change(d):
        def chunk(to):
            rel = lax.rem(to // 4 + xl, 2) * 4 + lax.rem(to, 4)
            k = kt[0, :, :, pl.ds(pl.multiple_of(rel * 256, 256), 256)].reshape(2048, 256)
            psend[to] = jnp.dot(d, k, preferred_element_type=F32).astype(BF16)

        def body(k, carry):
            to = ring_of(k)
            chunk(to)
            p_copy(to).start()
            return carry

        lax.fori_loop(0, 7, body, 0)
        chunk(e)

    def sum_change():
        def body(k, total):
            j = lax.rem(e + k, 8)
            remote(psend.at[j], precv.at[j], ps.at[j], pr.at[j], ring_dev(j)).wait_recv()
            return total + precv[j].astype(F32)

        return lax.fori_loop(1, 8, body, psend[e].astype(F32))

    def update_coefs(s, base):
        def body(k, carry):
            j = lax.rem(e + k, 8)
            remote(dall.at[s, j], dall.at[s, j], fs.at[s, j], fr.at[s, j], ring_dev(j)).wait_recv()
            return carry

        lax.fori_loop(1, 8, body, 0)
        lane = iota((16, 128), 1)
        pieces, cols = [], []
        for k in range(4):
            own = dall[s, xl * 4 + k]
            other = dall[s, (1 - xl) * 4 + k]
            pieces.append(jnp.where(lane < KEEP, own, other))
            cols.append(jnp.broadcast_to(places[k, s, 0:1], (128, 128)).T)
        lhs = split3(jnp.concatenate(pieces, axis=1))
        col = jnp.concatenate(cols, axis=0)

        def step(k, carry):
            at = pl.ds(pl.multiple_of(k * 512, 512), 512)
            base_lane = (k * 512).astype(F32)
            hot = []
            for i in range(4):
                lanes = iota((512, 128), 1).astype(F32) + (base_lane + i * 128.0)
                hot.append((col == lanes).astype(F32).astype(BF16))
            three = jnp.dot(lhs, jnp.concatenate(hot, axis=1), preferred_element_type=F32)
            coef_out[:, at] = base[:, at] + sum3(three)
            return carry

        lax.fori_loop(0, 8, step, 0)

    level(0, 0, 1)
    for s in range(2):
        for j in range(16):
            kt[s, j, 96:128, :] = jnp.zeros((32, 2048), BF16)
    level(0, 0, 2)
    level(0, 1, 1)
    level(0, 0, 3)
    level(0, 1, 2)
    tiles(0, 0, 0, 1)
    launch(1, 0)
    half_copy(1).wait_recv()
    launch(1, 1)
    level(0, 0, 4)
    for i in range(2):
        x_samples[i].wait_recv()
        hand[i].start()
    level(0, 1, 3)
    tiles(0, 0, 1, 3)
    level(1, 0, 1)
    level(1, 1, 1)
    x_rows[0].wait_recv()
    x_rows[1].wait_recv()
    weight_rows(1)
    wt[:, 1024:2048] = peer_wt[...]
    for i in range(2):
        hand_in[i].wait_recv()
    lax.fori_loop(1, 4, share_place, 0)
    tiles(0, 1, 0, 3)
    level(0, 1, 4)
    tiles(0, 0, 3, 4)
    tiles(0, 1, 3, 4)
    push_squares(0)
    gradient(0, wt[...])
    level(1, 0, 2)
    level(1, 1, 2)
    tiles(1, 0, 0, 1)
    tiles(1, 1, 0, 1)
    x_coef.wait_recv()
    make_delta(0)
    level(1, 0, 3)
    level(1, 1, 3)
    push_delta(0)
    tiles(1, 0, 1, 3)
    tiles(1, 1, 1, 2)
    change(wait_delta(0))
    level(1, 0, 4)
    level(1, 1, 4)
    tiles(1, 1, 2, 3)
    tiles(1, 0, 3, 4)
    chunk_at = pl.ds(pl.multiple_of(c * 256, 256), 256)
    pred = preds[:, chunk_at] + sum_change()

    def rel_to(to):
        return lax.rem(to // 4 + xl, 2) * 4 + c

    def w_copy(to):
        return remote(wt2.at[c], wt2.at[rel_to(to)], ws.at[to], wr.at[rel_to(to)], ring_dev(to))

    wt2[c] = (weights[:, chunk_at] * (targets[:, chunk_at] - pred)).astype(BF16)

    def push_w(k, carry):
        w_copy(ring_of(k)).start()
        return carry

    lax.fori_loop(0, 7, push_w, 0)
    pmid[c] = pred

    def q_copy(k):
        to = lax.rem(c + k, 4)
        return remote(pmid.at[c], pmid.at[c], qs.at[to], qr.at[c], (r, to))

    def push_q(k, carry):
        q_copy(k).start()
        return carry

    tiles(1, 1, 3, 4)
    push_squares(1)

    def wait_w(k, carry):
        j = lax.rem(c + k, 8)
        remote(wt2.at[j], wt2.at[j], ws.at[j], wr.at[j], ring_dev(j)).wait_recv()
        return carry

    lax.fori_loop(1, 8, wait_w, 0)
    gradient(1, jnp.concatenate([wt2[j] for j in range(8)], axis=1))
    lax.fori_loop(1, 4, push_q, 0)

    def wait_place(k, carry):
        j = lax.rem(c + k, 4)
        remote(place, places.at[j], ls.at[k], lr.at[j], (r, j)).wait_recv()
        return carry

    lax.fori_loop(1, 4, wait_place, 0)
    update_coefs(0, coefs)
    for s in range(2):
        half_copy(s).wait_send()
        for cp in started[s]:
            cp.wait_send()
    for cp in (*x_samples, *x_rows, x_coef, *hand):
        cp.wait_send()

    def drain_plane(s):
        def body(k, carry):
            j = lax.rem(me + k, 16)
            g_copy(s, j).wait_send()
            s_copy(s, j).wait_send()
            d_copy(s, j).wait_send()
            return carry

        lax.fori_loop(1, 16, body, 0)

    def drain_ring(k, carry):
        j = lax.rem(e + k, 8)
        f_copy(0, j).wait_send()
        p_copy(j).wait_send()
        w_copy(j).wait_send()
        return carry

    def drain_cent(k, carry):
        l_copy(k).wait_send()
        return carry

    drain_plane(0)
    lax.fori_loop(1, 8, drain_ring, 0)
    lax.fori_loop(1, 4, drain_cent, 0)
    make_delta(1)
    push_delta(1)
    d = wait_delta(1)

    def e_copy(rel, half, across_x):
        to_xl = xl if rel == 0 else 1 - xl
        to_hi = c // 2 if across_x == 0 else 1 - c // 2
        n = (rel * 2 + half) * 2 + across_x
        dev = (to_xl * 16 + me, to_hi * 2 + half)
        return remote(lsend.at[rel * 2 + half], lrecv.at[e], es.at[n], er.at[e], dev)

    for rel in range(2):
        for half in range(2):
            k = kt[1, :, :, rel * 1024 + half * 512 : rel * 1024 + half * 512 + 512].reshape(2048, 512)
            lsend[rel * 2 + half] = jnp.dot(d, k, preferred_element_type=F32).astype(BF16)
            e_copy(rel, half, 1).start()
            if rel == 1:
                e_copy(rel, half, 0).start()
            else:
                pl.when(core != half)(lambda half=half: e_copy(0, half, 0).start())
    lrecv[e] = lsend[core]
    update_coefs(1, coef_out)
    store_coef = pltpu.make_async_copy(coef_out, coef_hbm, loads.at[7])
    store_coef.start()
    def drain_last(k, carry):
        f_copy(1, lax.rem(e + k, 8)).wait_send()
        return carry

    def drain_mid(k, carry):
        q_copy(k).wait_send()
        return carry

    drain_plane(1)
    lax.fori_loop(1, 8, drain_last, 0)
    lax.fori_loop(1, 4, drain_mid, 0)

    def wait_q(k, carry):
        j = lax.rem(c + k, 4)
        remote(pmid.at[j], pmid.at[j], qs.at[j], qr.at[j], (r, j)).wait_recv()
        return carry

    lax.fori_loop(1, 4, wait_q, 0)

    def wait_e(k, carry):
        j = lax.rem(e + k, 8)
        remote(lrecv.at[j], lrecv.at[j], es.at[0], er.at[j], ring_dev(j)).wait_recv()
        return carry

    lax.fori_loop(1, 8, wait_e, 0)
    total = lrecv[0].astype(F32)
    for j in range(1, 8):
        total = total + lrecv[j].astype(F32)
    pend[core] = jnp.concatenate([pmid[core * 2], pmid[core * 2 + 1]], axis=1) + total
    final = remote(pend.at[core], pend.at[core], hs.at[2], hr.at[2], sibling)
    final.start()
    remote(pend.at[1 - core], pend.at[1 - core], hs.at[2], hr.at[2], sibling).wait_recv()
    pred_out[:, 0:512] = pend[0]
    pred_out[:, 512:1024] = pend[1]

    store_pred = pltpu.make_async_copy(pred_out, pred_hbm, loads.at[8])
    store_pred.start()
    for rel in range(2):
        for half in range(2):
            e_copy(rel, half, 1).wait_send()
            if rel == 1:
                e_copy(rel, half, 0).wait_send()
            else:
                pl.when(core != half)(lambda half=half: e_copy(0, half, 0).wait_send())
    final.wait_send()
    store_coef.wait()
    store_pred.wait()


def local(samples, weights, targets, predictions, centres, coefs, block_index):
    rows, depth = samples.shape
    pool = centres.shape[0]
    t = targets.shape[0]
    sharpness = 1.3 / math.sqrt(8.0 * depth)
    offset = 2.0 * depth * sharpness - 1.5 - 0.5 * math.log(rows * lax.axis_size("rows"))
    scale = sharpness * LOG2E
    shift = offset * LOG2E
    vmem = pl.BlockSpec(memory_space=pltpu.VMEM)
    hbm = pl.BlockSpec(memory_space=pl.ANY)
    sds = jax.ShapeDtypeStruct
    dma = pltpu.SemaphoreType.DMA
    pred, coef = pl.pallas_call(
        functools.partial(main_kernel, scale, shift),
        out_shape=(sds((t, rows), F32), sds((t, pool), F32)),
        in_specs=[hbm] * 7,
        out_specs=(hbm,) * 2,
        scratch_shapes=[
            pltpu.VMEM((t, rows), F32),
            pltpu.VMEM((t, pool), F32),
            pltpu.VMEM(block_index.shape, jnp.int32),
            pltpu.VMEM(centres.shape, BF16),
            pltpu.VMEM(coefs.shape, F32),
            pltpu.VMEM(samples.shape, BF16),
            pltpu.VMEM((1, rows), F32),
            pltpu.VMEM((t, rows), F32),
            pltpu.VMEM((t, rows), F32),
            pltpu.VMEM((256, pool), BF16),
            pltpu.VMEM((2, 96 - KEEP, depth), BF16),
            pltpu.VMEM((2, t, 128), F32),
            pltpu.VMEM((2, 8, 128), F32),
            pltpu.VMEM((t, rows), BF16),
            pltpu.VMEM((depth, rows), BF16),
            pltpu.VMEM((2, 16, 96, depth), BF16),
            pltpu.VMEM((depth, rows), BF16),
            pltpu.VMEM((2, t, 128), F32),
            pltpu.VMEM((4, 2, 8, 128), F32),
            pltpu.VMEM((t, 2 * rows), BF16),
            pltpu.VMEM((t, rows), BF16),
            pltpu.VMEM((2, 8, rows), F32),
            pltpu.VMEM((16, 2 * rows), BF16),
            pltpu.VMEM((2, 16, 128, 2 * rows), BF16),
            pltpu.VMEM((2, 16, t, 128), BF16),
            pltpu.VMEM((2, 16, t, 128), BF16),
            pltpu.VMEM((2, 16, 8, 128), F32),
            pltpu.VMEM((2, 16, 8, 128), F32),
            pltpu.VMEM((2, 16, t, 128), BF16),
            pltpu.VMEM((2, 8, t, 128), F32),
            pltpu.VMEM((8, t, 256), BF16),
            pltpu.VMEM((8, t, 256), BF16),
            pltpu.VMEM((4, t, 512), BF16),
            pltpu.VMEM((8, t, 512), BF16),
            pltpu.VMEM((8, t, 256), BF16),
            pltpu.VMEM((4, t, 256), F32),
            pltpu.VMEM((2, t, 512), F32),
            dma((9,)),
            dma((7,)), dma((7,)),
            dma((2, 30)), dma((2, 2, 16)),
            dma((2, 16)), dma((2, 16)),
            dma((2, 16)), dma((2, 16)),
            dma((2, 16)), dma((2, 16)),
            dma((2, 8)), dma((2, 8)),
            dma((8,)), dma((8,)),
            dma((8,)), dma((8,)),
            dma((8,)), dma((8,)),
            dma((4,)), dma((4,)),
            dma((4,)), dma((4,)),
            dma((3,)), dma((3,)),
        ],
        compiler_params=pltpu.CompilerParams(
            collective_id=0, has_side_effects=True, vmem_limit_bytes=60 * 2**20
        ),
    )(block_index, centres, coefs, samples, weights[None, :], targets, predictions)
    return coef, pred


def solution(mesh):
    in_specs = (
        P("rows", None),
        P("rows"),
        P(None, "rows"),
        P(None, "rows"),
        P("rows", None),
        P(None, "rows"),
        P(None, "cent"),
    )
    out_specs = (P(None, "rows"), P(None, "rows"))
    return jax.shard_map(local, mesh=mesh, in_specs=in_specs, out_specs=out_specs, check_vma=False)
```
